32 devices in a mesh: tok: 8 (over y, x, core), voc: 4 (over z).
Axes of the slice: x: 2, y: 2, z: 4, core: 2. Of those that a mesh axis runs over, the one named last changes fastest.
Arguments:
- student_hidden: bfloat16 [128, 2560], P('tok', 'voc'), may hold values from -72 to 72
- teacher_rows: bfloat16 [128, 4096], P('tok', 'voc'), may hold values from -72 to 72
- student_head: bfloat16 [2560, 8192], P(None, ('tok', 'voc')), may hold values from -0.375 to 0.375
- teacher_head: bfloat16 [4096, 8192], P(None, ('tok', 'voc')), may hold values from -0.25 to 0.25
- lengths: int32 [8], replicated, may hold values from 1 to 16, 80 in all
- route: int32 [128], replicated, may hold values from 0 to 127, each once
- sampled_ids: int32 [128], replicated, may hold values from 0 to 8191
- mix_flags: int32 [128], replicated, may hold values 0 or 1
Outputs:
- divergence: float32 [128], P('tok')
- head_grad: bfloat16 [2560, 8192], P(None, ('tok', 'voc'))
The draws below stay inside these ranges and needn't reach their ends.
Inputs may be any that keep to these rules, and one draw needn't show every extreme that they name: The lengths sum to 80; the largest is exactly 16. `route`: each trainer position appears once.
All inputs are finite; a program needn't handle non-finite values.
Results may differ from the reference program's by a relative error of at most 0.0052.
Values may be sent and summed in bfloat16 or wider, within the bound.
A program may use at most 64 MiB of HBM per device.

```python
import math
import jax
import jax.numpy as jnp
import numpy as np
from jax import lax

DS = 2560
DT = 4096
TOK_GRP = 16
TOKENS = 128
LIVE = 80
V = 8192
N_TOK = 8


def hidden_rows(key, width, shown_scale):
    values = jnp.clip(jax.random.normal(key, (TOKENS, width), jnp.float32), -6.0, 6.0)
    values = values * shown_scale
    return values.astype(jnp.bfloat16)


def draw_student_hidden(key, part):
    return hidden_rows(jax.random.fold_in(key, 11), DS, 0.5)


def draw_teacher_rows(key, part):
    return hidden_rows(jax.random.fold_in(key, 23), DT, 1.0)


def set_ends(array, rng, least, high):
    shape = array.shape
    place = [jax.random.randint(jax.random.fold_in(rng, axis), (), 0, shape[axis]) for axis in range(len(shape))]
    array = array.at[tuple(place)].set(least)
    longest = shape.index(max(shape))
    place[longest] = (place[longest] + 1) % shape[longest]
    return array.at[tuple(place)].set(high)


def level_of(rng, extent, pieces, least, high):
    def one(dim, parts):
        heights = jax.random.uniform(jax.random.fold_in(jax.random.fold_in(rng, 6), dim), (parts,), jnp.float32, least / len(pieces), high / len(pieces))
        return jnp.repeat(jnp.exp(heights), extent[dim] // parts).reshape((-1,) + (1,) * (len(extent) - dim - 1))

    factor_of = one(*pieces[0])
    for cut in pieces[1:]:
        factor_of = factor_of * one(*cut)
    return factor_of


def profile(count, total, most, slope):
    portions = [(1 << 20) // math.isqrt(grade ** slope) + 1 for grade in range(2, count + 1)]
    spare, counts = total - most - (count - 1), [1] * (count - 1)
    while spare > 0:
        candidates = [i for i in range(count - 1) if counts[i] < most]
        mass, remaining = sum([portions[i] for i in candidates]), spare
        for i in candidates:
            extra = min(most - counts[i], max(1, remaining * portions[i] // mass), spare)
            counts[i] = counts[i] + extra
            spare = spare - extra
    return np.array([most] + counts)


def uneven(stream_key, amount, total, reach, slope):
    if amount == 2:
        one = jax.random.randint(stream_key, (), max(1, total - reach), min(reach, total - 1) + 1)
        return jnp.stack([one, total - one])
    sizes = jnp.asarray(profile(amount, total, reach, slope), jnp.int32)
    couples = (amount - 1) // 2
    source_of, taker = sizes[1:1 + 2 * couples:2], sizes[2:2 + 2 * couples:2]
    slack = jnp.minimum(source_of - 1, reach - taker)
    moved = jax.random.randint(jax.random.fold_in(stream_key, 1), (couples,), 0, 1 << 20) % (slack + 1)
    sizes = sizes.at[1:1 + 2 * couples:2].set(source_of - moved).at[2:2 + 2 * couples:2].set(taker + moved)
    return sizes[jax.random.permutation(jax.random.fold_in(stream_key, 2), amount)]


def gaussian(stream_key, dims, spread, limit, split=(), kind=jnp.bfloat16):
    array = spread * jax.random.normal(stream_key, dims, jnp.float32)
    if split:
        array = array * level_of(stream_key, dims, split, -0.22, 0.18)
    return jnp.clip(array, -limit, limit).astype(kind)


def setup_inputs(seed: int = 0) -> dict:
    streams_of = jax.random.split(jax.random.key(seed), 9)
    student_hidden = draw_student_hidden(jax.random.fold_in(streams_of[8], 71), 0)
    teacher_rows = draw_teacher_rows(jax.random.fold_in(streams_of[8], 71), 0)
    student_head = gaussian(streams_of[2], (DS, V), (DS // 9) ** -0.5, 0.375, ((1, 32),))
    teacher_head = gaussian(streams_of[3], (DT, V), (DT // 9) ** -0.5, 0.25, ((1, 32),))
    lengths = uneven(streams_of[4], N_TOK, LIVE, TOK_GRP, 2).astype(jnp.int32)
    route = jax.random.permutation(streams_of[5], TOKENS).astype(jnp.int32)
    sampled_ids = set_ends(jax.random.randint(streams_of[6], (TOKENS,), 0, V), jax.random.fold_in(streams_of[6], 1), 0, V - 1).astype(jnp.int32)
    mix_flags = set_ends((jax.random.randint(streams_of[7], (TOKENS,), 0, 2) < 1).astype(jnp.int32), jax.random.fold_in(streams_of[7], 1), 0, 1)
    return dict(student_hidden=student_hidden, teacher_rows=teacher_rows, student_head=student_head, teacher_head=teacher_head, lengths=lengths, route=route, sampled_ids=sampled_ids, mix_flags=mix_flags)


def reference(student_hidden, teacher_rows, student_head, teacher_head, lengths, route, sampled_ids, mix_flags):
    position = jnp.arange(TOKENS, dtype=jnp.int32)
    live = ((position % TOK_GRP) < lengths[position // TOK_GRP]).astype(jnp.float32)
    teacher_hidden = jnp.zeros_like(teacher_rows).at[route].set(teacher_rows)
    student_logits = jnp.dot(student_hidden, student_head, preferred_element_type=jnp.float32)
    teacher_logits = jnp.dot(teacher_hidden, teacher_head, preferred_element_type=jnp.float32)
    log_student = jax.nn.log_softmax(student_logits, axis=-1)
    log_teacher = jax.nn.log_softmax(teacher_logits, axis=-1)
    probs = jnp.exp(log_student)
    gap = log_student - log_teacher
    kl_all = jnp.sum(probs * gap, axis=-1)
    student_pick = jnp.take_along_axis(log_student, sampled_ids[:, None], axis=1)[:, 0]
    teacher_pick = jnp.take_along_axis(log_teacher, sampled_ids[:, None], axis=1)[:, 0]
    mixed = 1.0 / (0.2 * jnp.exp(teacher_pick - student_pick) + 0.8)
    weight = jnp.where(mix_flags == 1, mixed, jnp.ones_like(mixed))
    divergence = live * kl_all
    dlogits = ((live * weight)[:, None] * probs * (gap - kl_all[:, None])).astype(jnp.bfloat16)
    head_grad = lax.dot_general(student_hidden, dlogits, (((0,), (0,)), ((), ())), preferred_element_type=jnp.float32)
    return divergence, head_grad.astype(jnp.bfloat16)
```

```python
import functools
import math

import jax
import jax.numpy as jnp
from jax import lax
from jax.experimental import pallas as pl
from jax.experimental.pallas import tpu as pltpu
from jax.sharding import PartitionSpec as P

MESH = pl.DeviceIdType.MESH
F32 = jnp.float32
BF16 = jnp.bfloat16


def grid_of(n_tok):
    cores = 2 if n_tok % 2 == 0 else 1
    chips = n_tok // cores
    wide = math.isqrt(chips)
    while chips % wide:
        wide -= 1
    return chips // wide, wide, cores


def partner(me, step, count):
    if count & (count - 1):
        return lax.rem(me + step, count)
    out = me
    bit = 1
    while bit < count:
        if step & bit:
            out = out + bit - 2 * bit * lax.rem(out // bit, 2)
        bit *= 2
    return out


def merge(block):
    row = lambda q: block[:, q:q + 1, :]
    ms, zs, mu, zu, acc, ps, pu = [row(q) for q in range(7)]
    top_s, top_u = jnp.max(ms, axis=0), jnp.max(mu, axis=0)
    ds, du = ms - top_s[None], mu - top_u[None]
    es = jnp.exp(ds)
    return (
        top_s,
        jnp.sum(zs * es, axis=0),
        top_u,
        jnp.sum(zu * jnp.exp(du), axis=0),
        jnp.sum(es * (acc + zs * (ds - du)), axis=0),
        jnp.sum(ps, axis=0),
        jnp.sum(pu, axis=0),
    )


def gather_kernel(
    n_tok, n_voc, hs, ht, ws, wt, lengths, route, ids, flags,
    rows_t_out, dl_out, div_out,
    bs, bt, vs, vt, stat1, stat2,
    send_z, recv_z, send_a, recv_a, send_b, recv_b, send_c, recv_c,
    send_1, recv_1, send_2, recv_2, loc,
):
    ny, nx, nc = grid_of(n_tok)
    tok, voc = lax.axis_index("tok"), lax.axis_index("voc")
    core = lax.rem(tok, nc)
    x = lax.rem(tok // nc, nx)
    y = tok // (nc * nx)
    tok_of = lambda yy, xx, cc: (yy * nx + xx) * nc + cc
    grp = hs.shape[0]
    tokens = grp * n_tok
    cols = ws.shape[1]
    first_col = (tok * n_voc + voc) * cols

    own = [
        pltpu.make_async_copy(hs, bs.at[voc, y, x, core], loc.at[0]),
        pltpu.make_async_copy(ht, bt.at[voc, y, x, core], loc.at[1]),
        pltpu.make_async_copy(ws, vs, loc.at[2]),
        pltpu.make_async_copy(wt, vt, loc.at[3]),
    ]
    for copy in own:
        copy.start()

    barrier = pltpu.get_barrier_semaphore()
    for i in range(1, n_tok):
        pl.semaphore_signal(
            barrier, inc=1, device_id=(lax.rem(tok + i, n_tok), voc), device_id_type=MESH
        )
    for j in range(1, n_voc):
        pl.semaphore_signal(
            barrier, inc=1, device_id=(tok, partner(voc, j, n_voc)), device_id_type=MESH
        )
    pl.semaphore_wait(barrier, n_tok + n_voc - 2)

    started = []

    def push(src, dst, ssem, rsem, device):
        copy = pltpu.make_async_remote_copy(
            src_ref=src, dst_ref=dst, send_sem=ssem, recv_sem=rsem,
            device_id=device, device_id_type=MESH,
        )
        copy.start()
        started.append(copy)

    def arrived(dst, ssem, rsem, device):
        pltpu.make_async_remote_copy(
            src_ref=dst, dst_ref=dst, send_sem=ssem, recv_sem=rsem,
            device_id=device, device_id_type=MESH,
        ).wait_recv()

    bufs = (bt, bs)
    srcs = (ht, hs)

    def send_along_z(j):
        to = partner(voc, j, n_voc)
        for q in range(2):
            push(srcs[q], bufs[q].at[voc, y, x, core],
                 send_z.at[q, to], recv_z.at[q, voc], (tok, to))

    def wait_along_z(j):
        k = partner(voc, j, n_voc)
        for q in range(2):
            arrived(bufs[q].at[k, y, x, core], send_z.at[q, k], recv_z.at[q, k], (tok, k))

    def first_hop(j):
        k = partner(voc, j, n_voc)
        for i in range(1, nx):
            to = lax.rem(x + i, nx)
            push(ht if j == 0 else bt.at[k, y, x, core], bt.at[k, y, x, core],
                 send_a.at[0, k, to], recv_a.at[0, k, x], (tok_of(y, to, core), voc))
        for i in range(1, ny):
            to = lax.rem(y + i, ny)
            push(hs if j == 0 else bs.at[k, y, x, core], bs.at[k, y, x, core],
                 send_a.at[1, k, to], recv_a.at[1, k, y], (tok_of(to, x, core), voc))

    def wait_first(j):
        k = partner(voc, j, n_voc)
        for i in range(1, nx):
            at = lax.rem(x + i, nx)
            arrived(bt.at[k, y, at, core], send_a.at[0, k, at], recv_a.at[0, k, at],
                    (tok_of(y, at, core), voc))
        for i in range(1, ny):
            at = lax.rem(y + i, ny)
            arrived(bs.at[k, at, x, core], send_a.at[1, k, at], recv_a.at[1, k, at],
                    (tok_of(at, x, core), voc))

    def second_hop(j):
        k = partner(voc, j, n_voc)
        for i in range(1, ny):
            to = lax.rem(y + i, ny)
            push(bt.at[k, y, :, core], bt.at[k, y, :, core],
                 send_b.at[0, k, to], recv_b.at[0, k, y], (tok_of(to, x, core), voc))
        for i in range(1, nx):
            to = lax.rem(x + i, nx)
            push(bs.at[k, :, x, core], bs.at[k, :, x, core],
                 send_b.at[1, k, to], recv_b.at[1, k, x], (tok_of(y, to, core), voc))

    def wait_second(j):
        k = partner(voc, j, n_voc)
        for i in range(1, ny):
            at = lax.rem(y + i, ny)
            arrived(bt.at[k, at, :, core], send_b.at[0, k, at], recv_b.at[0, k, at],
                    (tok_of(at, x, core), voc))
        for i in range(1, nx):
            at = lax.rem(x + i, nx)
            arrived(bs.at[k, :, at, core], send_b.at[1, k, at], recv_b.at[1, k, at],
                    (tok_of(y, at, core), voc))

    def core_hop(j):
        k = partner(voc, j, n_voc)
        for i in range(1, nc):
            to = lax.rem(core + i, nc)
            for q in range(2):
                push(bufs[q].at[k, :, :, core], bufs[q].at[k, :, :, core],
                     send_c.at[q, k], recv_c.at[q, k], (tok_of(y, x, to), voc))

    def wait_core(j):
        k = partner(voc, j, n_voc)
        for i in range(1, nc):
            at = lax.rem(core + i, nc)
            for q in range(2):
                arrived(bufs[q].at[k, :, :, at], send_c.at[q, k], recv_c.at[q, k],
                        (tok_of(y, x, at), voc))

    def product(j):
        k = partner(voc, j, n_voc)
        out = []
        for buf, head in ((bt, vt), (bs, vs)):
            depth = buf.shape[-1]
            rows = buf[k].reshape(tokens, depth)
            part = head[pl.ds(pl.multiple_of(k * depth, depth), depth), :]
            out.append(jnp.dot(rows, part, preferred_element_type=F32))
        return out

    u = jnp.zeros((tokens, cols), F32)
    s = jnp.zeros((tokens, cols), F32)
    for j in range(n_voc + 3):
        if j == 0:
            if n_voc > 1:
                send_along_z(1)
            first_hop(0)
            for i in range(2, n_voc):
                send_along_z(i)
            for copy in own:
                copy.wait()
        elif j < n_voc:
            wait_along_z(j)
            first_hop(j)
        if 0 <= j - 1 < n_voc:
            wait_first(j - 1)
            second_hop(j - 1)
        if 0 <= j - 2 < n_voc:
            wait_second(j - 2)
            core_hop(j - 2)
        if 0 <= j - 3 < n_voc:
            wait_core(j - 3)
            du, ds = product(j - 3)
            u = u + du
            s = s + ds

    perm = (lax.broadcasted_iota(jnp.int32, (tokens, tokens), 0) == route[...]).astype(BF16)
    hi = u.astype(BF16)
    rest = u - hi.astype(F32)
    mid = rest.astype(BF16)
    low = (rest - mid.astype(F32)).astype(BF16)
    move = lambda part: jnp.dot(perm, part, preferred_element_type=F32)
    u = (move(hi) + move(mid)) + move(low)
    s, u = s.T, u.T

    entry = lax.broadcasted_iota(jnp.int32, (cols, tokens), 0) + first_col
    picked = entry == ids[...]
    ms = jnp.max(s, axis=0, keepdims=True)
    mu = jnp.max(u, axis=0, keepdims=True)
    cs, cu = s - ms, u - mu
    es = jnp.exp(cs)
    total = lambda a: jnp.sum(a, axis=0, keepdims=True)
    mine = (
        ms, total(es), mu, total(jnp.exp(cu)), total(es * (cs - cu)),
        total(jnp.where(picked, s, 0.0)), total(jnp.where(picked, u, 0.0)),
    )

    def put(slots, at, values):
        for q, value in enumerate(values):
            slots[at, q:q + 1, :] = value
        slots[at, 7:8, :] = jnp.zeros_like(values[0])

    put(stat1, tok, mine)
    for i in range(1, n_tok):
        to = lax.rem(tok + i, n_tok)
        push(stat1.at[tok], stat1.at[tok], send_1.at[to], recv_1.at[tok], (to, voc))

    for k in range(n_voc):
        rows_t_out[k] = bs[k].reshape(tokens, hs.shape[1]).T

    for i in range(1, n_tok):
        at = lax.rem(tok + i, n_tok)
        arrived(stat1.at[at], send_1.at[at], recv_1.at[at], (at, voc))
    put(stat2, voc, merge(stat1[...]))
    for j in range(1, n_voc):
        to = partner(voc, j, n_voc)
        push(stat2.at[voc], stat2.at[voc], send_2.at[to], recv_2.at[voc], (tok, to))
    position = lax.broadcasted_iota(jnp.int32, (1, tokens), 1)
    limit = jnp.zeros((1, tokens), jnp.int32)
    for w in range(n_tok):
        limit = jnp.where(position // grp == w, lengths[w], limit)
    live = (lax.rem(position, grp) < limit).astype(F32)
    for j in range(1, n_voc):
        at = partner(voc, j, n_voc)
        arrived(stat2.at[at], send_2.at[at], recv_2.at[at], (tok, at))
    ms, zs, mu, zu, acc, ps, pu = merge(stat2[...])
    log_zs, log_zu = jnp.log(zs), jnp.log(zu)
    kl = acc / zs - log_zs + log_zu
    mixed = 1.0 / (0.2 * jnp.exp((pu - mu - log_zu) - (ps - ms - log_zs)) + 0.8)
    weight = jnp.where(flags[...] == 1, mixed, 1.0)
    ls = s - ms - log_zs
    gap = ls - (u - mu - log_zu)
    dl = (live * weight) * jnp.exp(ls) * (gap - kl)
    dl_out[...] = dl.T.astype(BF16)
    div_out[...] = live * kl
    for copy in started:
        copy.wait_send()


def grad_kernel(n_tok, rows_t, dl, div_all, grad, div):
    grad[...] = jnp.dot(rows_t[0], dl[...], preferred_element_type=F32).astype(BF16)
    tokens = div_all.shape[1]
    grp = tokens // n_tok
    first = lax.axis_index("tok") * grp
    at = lax.broadcasted_iota(jnp.int32, (grp, tokens), 0) + first
    here = at == lax.broadcasted_iota(jnp.int32, (grp, tokens), 1)
    div[...] = jnp.sum(jnp.where(here, div_all[...], 0.0), axis=1, keepdims=True)


def on_device(
    n_tok, n_voc, student_hidden, teacher_rows, student_head, teacher_head,
    lengths, route, sampled_ids, mix_flags,
):
    grp, fs = student_hidden.shape
    ft = teacher_rows.shape[1]
    tokens = grp * n_tok
    ds, cols = student_head.shape
    dt = teacher_head.shape[0]
    ny, nx, nc = grid_of(n_tok)
    side = max(nx, ny)
    dma = pltpu.SemaphoreType.DMA
    anywhere = pl.BlockSpec(memory_space=pl.ANY)
    vmem = pl.BlockSpec(memory_space=pltpu.VMEM)
    line = lambda a: a.reshape(1, tokens)
    rows_t, dl, div_all = pl.pallas_call(
        functools.partial(gather_kernel, n_tok, n_voc),
        out_shape=(
            jax.ShapeDtypeStruct((n_voc, fs, tokens), BF16),
            jax.ShapeDtypeStruct((tokens, cols), BF16),
            jax.ShapeDtypeStruct((1, tokens), F32),
        ),
        in_specs=[anywhere] * 4 + [pl.BlockSpec(memory_space=pltpu.SMEM)] + [vmem] * 3,
        out_specs=(vmem, vmem, vmem),
        scratch_shapes=[
            pltpu.VMEM((n_voc, ny, nx, nc, grp, fs), BF16),
            pltpu.VMEM((n_voc, ny, nx, nc, grp, ft), BF16),
            pltpu.VMEM((ds, cols), BF16),
            pltpu.VMEM((dt, cols), BF16),
            pltpu.VMEM((n_tok, 8, tokens), F32),
            pltpu.VMEM((n_voc, 8, tokens), F32),
            dma((2, n_voc)), dma((2, n_voc)),
            dma((2, n_voc, side)), dma((2, n_voc, side)),
            dma((2, n_voc, side)), dma((2, n_voc, side)),
            dma((2, n_voc)), dma((2, n_voc)),
            dma((n_tok,)), dma((n_tok,)),
            dma((n_voc,)), dma((n_voc,)),
            dma((4,)),
        ],
        compiler_params=pltpu.CompilerParams(
            collective_id=0, has_side_effects=True, vmem_limit_bytes=40 << 20
        ),
        name="gather_and_softmax",
    )(
        student_hidden, teacher_rows, student_head, teacher_head,
        lengths, line(route), line(sampled_ids), line(mix_flags),
    )
    grad, div = pl.pallas_call(
        functools.partial(grad_kernel, n_tok),
        grid=(n_voc,),
        out_shape=(
            jax.ShapeDtypeStruct((ds, cols), BF16),
            jax.ShapeDtypeStruct((grp, 1), F32),
        ),
        in_specs=[
            pl.BlockSpec((1, fs, tokens), lambda i: (i, 0, 0)),
            pl.BlockSpec((tokens, cols), lambda i: (0, 0)),
            pl.BlockSpec((1, tokens), lambda i: (0, 0)),
        ],
        out_specs=(
            pl.BlockSpec((fs, cols), lambda i: (i, 0)),
            pl.BlockSpec((grp, 1), lambda i: (0, 0)),
        ),
        name="head_grad",
    )(rows_t, dl, div_all)
    return div.reshape(grp), grad


def solution(mesh):
    in_specs = (
        P("tok", "voc"),
        P("tok", "voc"),
        P(None, ("tok", "voc")),
        P(None, ("tok", "voc")),
        P(),
        P(),
        P(),
        P(),
    )
    out_specs = (P("tok"), P(None, ("tok", "voc")))
    body = functools.partial(on_device, mesh.shape["tok"], mesh.shape["voc"])
    return jax.shard_map(body, mesh=mesh, in_specs=in_specs, out_specs=out_specs, check_vma=False)
```

```python
import functools
import math

import jax
import jax.numpy as jnp
from jax import lax
from jax.experimental import pallas as pl
from jax.experimental.pallas import tpu as pltpu
from jax.sharding import PartitionSpec as P

MESH = pl.DeviceIdType.MESH
F32 = jnp.float32
BF16 = jnp.bfloat16


def grid_of(n_tok):
    cores = 2 if n_tok % 2 == 0 else 1
    chips = n_tok // cores
    wide = math.isqrt(chips)
    while chips % wide:
        wide -= 1
    return chips // wide, wide, cores


def partner(me, step, count):
    if count & (count - 1):
        return lax.rem(me + step, count)
    out = me
    bit = 1
    while bit < count:
        if step & bit:
            out = out + bit - 2 * bit * lax.rem(out // bit, 2)
        bit *= 2
    return out


def merge(block):
    row = lambda q: block[:, q:q + 1, :]
    ms, zs, mu, zu, acc, ps, pu = [row(q) for q in range(7)]
    top_s, top_u = jnp.max(ms, axis=0), jnp.max(mu, axis=0)
    ds, du = ms - top_s[None], mu - top_u[None]
    es = jnp.exp(ds)
    return (
        top_s,
        jnp.sum(zs * es, axis=0),
        top_u,
        jnp.sum(zu * jnp.exp(du), axis=0),
        jnp.sum(es * (acc + zs * (ds - du)), axis=0),
        jnp.sum(ps, axis=0),
        jnp.sum(pu, axis=0),
    )


def gather_kernel(
    n_tok, n_voc, hs, ht, ws, wt, lengths_in, route_in, ids_in, flags_in,
    rows_t_out, dl_out, div_out,
    lengths, route, ids, flags, bs, bt, vs, vt, stat1, stat2,
    send_z, recv_z, send_a, recv_a, send_b, recv_b, send_c, recv_c,
    send_1, recv_1, send_2, recv_2, loc,
):
    ny, nx, nc = grid_of(n_tok)
    tok, voc = lax.axis_index("tok"), lax.axis_index("voc")
    core = lax.rem(tok, nc)
    x = lax.rem(tok // nc, nx)
    y = tok // (nc * nx)
    tok_of = lambda yy, xx, cc: (yy * nx + xx) * nc + cc
    grp = hs.shape[0]
    tokens = grp * n_tok
    cols = ws.shape[1]
    first_col = (tok * n_voc + voc) * cols

    own = [
        pltpu.make_async_copy(hs, bs.at[voc, y, x, core], loc.at[0]),
        pltpu.make_async_copy(ht, bt.at[voc, y, x, core], loc.at[1]),
        pltpu.make_async_copy(ws, vs, loc.at[2]),
        pltpu.make_async_copy(wt, vt, loc.at[3]),
        pltpu.make_async_copy(lengths_in, lengths, loc.at[4]),
        pltpu.make_async_copy(route_in, route, loc.at[5]),
        pltpu.make_async_copy(ids_in, ids, loc.at[6]),
        pltpu.make_async_copy(flags_in, flags, loc.at[7]),
    ]
    for copy in own:
        copy.start()

    barrier = pltpu.get_barrier_semaphore()
    for i in range(1, n_tok):
        pl.semaphore_signal(
            barrier, inc=1, device_id=(lax.rem(tok + i, n_tok), voc), device_id_type=MESH
        )
    for j in range(1, n_voc):
        pl.semaphore_signal(
            barrier, inc=1, device_id=(tok, partner(voc, j, n_voc)), device_id_type=MESH
        )
    pl.semaphore_wait(barrier, n_tok + n_voc - 2)

    started = []

    def push(src, dst, ssem, rsem, device):
        copy = pltpu.make_async_remote_copy(
            src_ref=src, dst_ref=dst, send_sem=ssem, recv_sem=rsem,
            device_id=device, device_id_type=MESH,
        )
        copy.start()
        started.append(copy)

    def arrived(dst, ssem, rsem, device):
        pltpu.make_async_remote_copy(
            src_ref=dst, dst_ref=dst, send_sem=ssem, recv_sem=rsem,
            device_id=device, device_id_type=MESH,
        ).wait_recv()

    bufs = (bt, bs)
    srcs = (ht, hs)

    def send_along_z(j):
        to = partner(voc, j, n_voc)
        for q in range(2):
            push(srcs[q], bufs[q].at[voc, y, x, core],
                 send_z.at[q, to], recv_z.at[q, voc], (tok, to))

    def wait_along_z(j):
        k = partner(voc, j, n_voc)
        for q in range(2):
            arrived(bufs[q].at[k, y, x, core], send_z.at[q, k], recv_z.at[q, k], (tok, k))

    def first_hop(j):
        k = partner(voc, j, n_voc)
        for i in range(1, nx):
            to = lax.rem(x + i, nx)
            push(ht if j == 0 else bt.at[k, y, x, core], bt.at[k, y, x, core],
                 send_a.at[0, k, to], recv_a.at[0, k, x], (tok_of(y, to, core), voc))
        for i in range(1, ny):
            to = lax.rem(y + i, ny)
            push(hs if j == 0 else bs.at[k, y, x, core], bs.at[k, y, x, core],
                 send_a.at[1, k, to], recv_a.at[1, k, y], (tok_of(to, x, core), voc))

    def wait_first(j):
        k = partner(voc, j, n_voc)
        for i in range(1, nx):
            at = lax.rem(x + i, nx)
            arrived(bt.at[k, y, at, core], send_a.at[0, k, at], recv_a.at[0, k, at],
                    (tok_of(y, at, core), voc))
        for i in range(1, ny):
            at = lax.rem(y + i, ny)
            arrived(bs.at[k, at, x, core], send_a.at[1, k, at], recv_a.at[1, k, at],
                    (tok_of(at, x, core), voc))

    def second_hop(j):
        k = partner(voc, j, n_voc)
        for i in range(1, ny):
            to = lax.rem(y + i, ny)
            push(bt.at[k, y, :, core], bt.at[k, y, :, core],
                 send_b.at[0, k, to], recv_b.at[0, k, y], (tok_of(to, x, core), voc))
        for i in range(1, nx):
            to = lax.rem(x + i, nx)
            push(bs.at[k, :, x, core], bs.at[k, :, x, core],
                 send_b.at[1, k, to], recv_b.at[1, k, x], (tok_of(y, to, core), voc))

    def wait_second(j):
        k = partner(voc, j, n_voc)
        for i in range(1, ny):
            at = lax.rem(y + i, ny)
            arrived(bt.at[k, at, :, core], send_b.at[0, k, at], recv_b.at[0, k, at],
                    (tok_of(at, x, core), voc))
        for i in range(1, nx):
            at = lax.rem(x + i, nx)
            arrived(bs.at[k, :, at, core], send_b.at[1, k, at], recv_b.at[1, k, at],
                    (tok_of(y, at, core), voc))

    def core_hop(j):
        k = partner(voc, j, n_voc)
        for i in range(1, nc):
            to = lax.rem(core + i, nc)
            for q in range(2):
                push(bufs[q].at[k, :, :, core], bufs[q].at[k, :, :, core],
                     send_c.at[q, k], recv_c.at[q, k], (tok_of(y, x, to), voc))

    def wait_core(j):
        k = partner(voc, j, n_voc)
        for i in range(1, nc):
            at = lax.rem(core + i, nc)
            for q in range(2):
                arrived(bufs[q].at[k, :, :, at], send_c.at[q, k], recv_c.at[q, k],
                        (tok_of(y, x, at), voc))

    def product(j):
        k = partner(voc, j, n_voc)
        out = []
        for buf, head in ((bt, vt), (bs, vs)):
            depth = buf.shape[-1]
            rows = buf[k].reshape(tokens, depth)
            part = head[pl.ds(pl.multiple_of(k * depth, depth), depth), :]
            out.append(jnp.dot(rows, part, preferred_element_type=F32))
        return out

    u = jnp.zeros((tokens, cols), F32)
    s = jnp.zeros((tokens, cols), F32)
    for j in range(n_voc + 3):
        if j == 0:
            if n_voc > 1:
                send_along_z(1)
            first_hop(0)
            for i in range(2, n_voc):
                send_along_z(i)
            for copy in own:
                copy.wait()
        elif j < n_voc:
            wait_along_z(j)
            first_hop(j)
        if 0 <= j - 1 < n_voc:
            wait_first(j - 1)
            second_hop(j - 1)
        if 0 <= j - 2 < n_voc:
            wait_second(j - 2)
            core_hop(j - 2)
        if 0 <= j - 3 < n_voc:
            wait_core(j - 3)
            du, ds = product(j - 3)
            u = u + du
            s = s + ds

    perm = (lax.broadcasted_iota(jnp.int32, (tokens, tokens), 0) == route[...]).astype(BF16)
    hi = u.astype(BF16)
    rest = u - hi.astype(F32)
    mid = rest.astype(BF16)
    low = (rest - mid.astype(F32)).astype(BF16)
    move = lambda part: jnp.dot(perm, part, preferred_element_type=F32)
    u = (move(hi) + move(mid)) + move(low)
    s, u = s.T, u.T

    entry = lax.broadcasted_iota(jnp.int32, (cols, tokens), 0) + first_col
    picked = entry == ids[...]
    ms = jnp.max(s, axis=0, keepdims=True)
    mu = jnp.max(u, axis=0, keepdims=True)
    cs, cu = s - ms, u - mu
    es = jnp.exp(cs)
    total = lambda a: jnp.sum(a, axis=0, keepdims=True)
    mine = (
        ms, total(es), mu, total(jnp.exp(cu)), total(es * (cs - cu)),
        total(jnp.where(picked, s, 0.0)), total(jnp.where(picked, u, 0.0)),
    )

    def put(slots, at, values):
        for q, value in enumerate(values):
            slots[at, q:q + 1, :] = value
        slots[at, 7:8, :] = jnp.zeros_like(values[0])

    put(stat1, tok, mine)
    for i in range(1, n_tok):
        to = lax.rem(tok + i, n_tok)
        push(stat1.at[tok], stat1.at[tok], send_1.at[to], recv_1.at[tok], (to, voc))

    for k in range(n_voc):
        rows_t_out[k] = bs[k].reshape(tokens, hs.shape[1]).T

    for i in range(1, n_tok):
        at = lax.rem(tok + i, n_tok)
        arrived(stat1.at[at], send_1.at[at], recv_1.at[at], (at, voc))
    put(stat2, voc, merge(stat1[...]))
    for j in range(1, n_voc):
        to = partner(voc, j, n_voc)
        push(stat2.at[voc], stat2.at[voc], send_2.at[to], recv_2.at[voc], (tok, to))
    position = lax.broadcasted_iota(jnp.int32, (1, tokens), 1)
    limit = jnp.zeros((1, tokens), jnp.int32)
    for w in range(n_tok):
        limit = jnp.where(position // grp == w, lengths[w], limit)
    live = (lax.rem(position, grp) < limit).astype(F32)
    for j in range(1, n_voc):
        at = partner(voc, j, n_voc)
        arrived(stat2.at[at], send_2.at[at], recv_2.at[at], (tok, at))
    ms, zs, mu, zu, acc, ps, pu = merge(stat2[...])
    log_zs, log_zu = jnp.log(zs), jnp.log(zu)
    kl = acc / zs - log_zs + log_zu
    mixed = 1.0 / (0.2 * jnp.exp((pu - mu - log_zu) - (ps - ms - log_zs)) + 0.8)
    weight = jnp.where(flags[...] == 1, mixed, 1.0)
    ls = s - ms - log_zs
    gap = ls - (u - mu - log_zu)
    dl = (live * weight) * jnp.exp(ls) * (gap - kl)
    dl_out[...] = dl.T.astype(BF16)
    div_out[...] = live * kl
    for copy in started:
        copy.wait_send()


def grad_kernel(n_tok, rows_t, dl, div_all, grad, div, made, sems):
    n_voc, fs, tokens = rows_t.shape
    copies = []
    for k in range(n_voc):
        made[k] = jnp.dot(rows_t[k], dl[...], preferred_element_type=F32).astype(BF16)
        copies.append(pltpu.make_async_copy(made.at[k], grad.at[pl.ds(k * fs, fs)], sems.at[k]))
        copies[-1].start()
    grp = tokens // n_tok
    shift = lax.rem(tokens - lax.axis_index("tok") * grp, tokens)
    turned = pltpu.roll(jnp.broadcast_to(div_all[...], (8, tokens)), shift, 1)
    div[...] = turned[0:1, :grp]
    for copy in copies:
        copy.wait()


def on_device(
    n_tok, n_voc, student_hidden, teacher_rows, student_head, teacher_head,
    lengths, route, sampled_ids, mix_flags,
):
    grp, fs = student_hidden.shape
    ft = teacher_rows.shape[1]
    tokens = grp * n_tok
    ds, cols = student_head.shape
    dt = teacher_head.shape[0]
    ny, nx, nc = grid_of(n_tok)
    side = max(nx, ny)
    dma = pltpu.SemaphoreType.DMA
    hbm = pl.BlockSpec(memory_space=pltpu.HBM)
    vmem = pl.BlockSpec(memory_space=pltpu.VMEM)
    line = lambda a: a.reshape(1, tokens)
    rows_t, dl, div_all = pl.pallas_call(
        functools.partial(gather_kernel, n_tok, n_voc),
        out_shape=(
            jax.ShapeDtypeStruct((n_voc, fs, tokens), BF16),
            jax.ShapeDtypeStruct((tokens, cols), BF16),
            jax.ShapeDtypeStruct((1, tokens), F32),
        ),
        in_specs=[hbm] * 8,
        out_specs=(vmem, vmem, vmem),
        scratch_shapes=[
            pltpu.SMEM(lengths.shape, jnp.int32),
            pltpu.VMEM((1, tokens), jnp.int32),
            pltpu.VMEM((1, tokens), jnp.int32),
            pltpu.VMEM((1, tokens), jnp.int32),
            pltpu.VMEM((n_voc, ny, nx, nc, grp, fs), BF16),
            pltpu.VMEM((n_voc, ny, nx, nc, grp, ft), BF16),
            pltpu.VMEM((ds, cols), BF16),
            pltpu.VMEM((dt, cols), BF16),
            pltpu.VMEM((n_tok, 8, tokens), F32),
            pltpu.VMEM((n_voc, 8, tokens), F32),
            dma((2, n_voc)), dma((2, n_voc)),
            dma((2, n_voc, side)), dma((2, n_voc, side)),
            dma((2, n_voc, side)), dma((2, n_voc, side)),
            dma((2, n_voc)), dma((2, n_voc)),
            dma((n_tok,)), dma((n_tok,)),
            dma((n_voc,)), dma((n_voc,)),
            dma((8,)),
        ],
        compiler_params=pltpu.CompilerParams(
            collective_id=0, has_side_effects=True, vmem_limit_bytes=40 << 20
        ),
        name="gather_and_softmax",
    )(
        *[pltpu.with_memory_space_constraint(a, pltpu.HBM) for a in (
            student_hidden, teacher_rows, student_head, teacher_head,
            lengths, line(route), line(sampled_ids), line(mix_flags),
        )]
    )
    grad, div = pl.pallas_call(
        functools.partial(grad_kernel, n_tok),
        out_shape=(
            jax.ShapeDtypeStruct((ds, cols), BF16),
            jax.ShapeDtypeStruct((1, grp), F32),
        ),
        in_specs=[vmem] * 3,
        out_specs=(hbm, vmem),
        scratch_shapes=[pltpu.VMEM((n_voc, fs, cols), BF16), dma((n_voc,))],
        compiler_params=pltpu.CompilerParams(vmem_limit_bytes=12 << 20),
        name="head_grad",
    )(rows_t, dl, div_all)
    return div.reshape(grp), grad


def solution(mesh):
    in_specs = (
        P("tok", "voc"),
        P("tok", "voc"),
        P(None, ("tok", "voc")),
        P(None, ("tok", "voc")),
        P(),
        P(),
        P(),
        P(),
    )
    out_specs = (P("tok"), P(None, ("tok", "voc")))
    body = functools.partial(on_device, mesh.shape["tok"], mesh.shape["voc"])
    return jax.shard_map(body, mesh=mesh, in_specs=in_specs, out_specs=out_specs, check_vma=False)
```

```python
import functools
import math

import jax
import jax.numpy as jnp
from jax import lax
from jax.experimental import pallas as pl
from jax.experimental.pallas import tpu as pltpu
from jax.sharding import PartitionSpec as P

MESH = pl.DeviceIdType.MESH
F32 = jnp.float32
BF16 = jnp.bfloat16


def grid_of(n_tok):
    cores = 2 if n_tok % 2 == 0 else 1
    chips = n_tok // cores
    wide = math.isqrt(chips)
    while chips % wide:
        wide -= 1
    return chips // wide, wide, cores


def partner(me, step, count):
    if count & (count - 1):
        return lax.rem(me + step, count)
    out = me
    bit = 1
    while bit < count:
        if step & bit:
            out = out + bit - 2 * bit * lax.rem(out // bit, 2)
        bit *= 2
    return out


def merge(block):
    row = lambda q: block[:, q:q + 1, :]
    ms, zs, mu, zu, acc, ps, pu = [row(q) for q in range(7)]
    top_s, top_u = jnp.max(ms, axis=0), jnp.max(mu, axis=0)
    ds, du = ms - top_s[None], mu - top_u[None]
    es = jnp.exp(ds)
    return (
        top_s,
        jnp.sum(zs * es, axis=0),
        top_u,
        jnp.sum(zu * jnp.exp(du), axis=0),
        jnp.sum(es * (acc + zs * (ds - du)), axis=0),
        jnp.sum(ps, axis=0),
        jnp.sum(pu, axis=0),
    )


def gather_kernel(
    n_tok, n_voc, hs, ht, ws, wt, lengths_in, route_in, ids_in, flags_in,
    rows_t_out, dl_out, div_out,
    lengths, route, ids, flags, bs, bt, vs, vt, stat1, stat2,
    send_z, recv_z, send_a, recv_a, send_b, recv_b, send_c, recv_c,
    send_1, recv_1, send_2, recv_2, loc,
):
    ny, nx, nc = grid_of(n_tok)
    tok, voc = lax.axis_index("tok"), lax.axis_index("voc")
    core = lax.rem(tok, nc)
    x = lax.rem(tok // nc, nx)
    y = tok // (nc * nx)
    tok_of = lambda yy, xx, cc: (yy * nx + xx) * nc + cc
    grp = hs.shape[0]
    tokens = grp * n_tok
    cols = ws.shape[1]
    first_col = (tok * n_voc + voc) * cols

    own = [
        pltpu.make_async_copy(hs, bs.at[voc, y, x, core], loc.at[0]),
        pltpu.make_async_copy(ht, bt.at[voc, y, x, core], loc.at[1]),
        pltpu.make_async_copy(ws, vs, loc.at[2]),
        pltpu.make_async_copy(wt, vt, loc.at[3]),
        pltpu.make_async_copy(lengths_in, lengths, loc.at[4]),
        pltpu.make_async_copy(route_in, route, loc.at[5]),
        pltpu.make_async_copy(ids_in, ids, loc.at[6]),
        pltpu.make_async_copy(flags_in, flags, loc.at[7]),
    ]
    for copy in own:
        copy.start()

    barrier = pltpu.get_barrier_semaphore()
    for i in range(1, n_tok):
        pl.semaphore_signal(
            barrier, inc=1, device_id=(lax.rem(tok + i, n_tok), voc), device_id_type=MESH
        )
    for j in range(1, n_voc):
        pl.semaphore_signal(
            barrier, inc=1, device_id=(tok, partner(voc, j, n_voc)), device_id_type=MESH
        )
    pl.semaphore_wait(barrier, n_tok + n_voc - 2)

    started = []

    def push(src, dst, ssem, rsem, device):
        copy = pltpu.make_async_remote_copy(
            src_ref=src, dst_ref=dst, send_sem=ssem, recv_sem=rsem,
            device_id=device, device_id_type=MESH,
        )
        copy.start()
        started.append(copy)

    def arrived(dst, ssem, rsem, device):
        pltpu.make_async_remote_copy(
            src_ref=dst, dst_ref=dst, send_sem=ssem, recv_sem=rsem,
            device_id=device, device_id_type=MESH,
        ).wait_recv()

    bufs = (bt, bs)
    srcs = (ht, hs)

    def send_along_z(j):
        to = partner(voc, j, n_voc)
        for q in range(2):
            push(srcs[q], bufs[q].at[voc, y, x, core],
                 send_z.at[q, to], recv_z.at[q, voc], (tok, to))

    def wait_along_z(j):
        k = partner(voc, j, n_voc)
        for q in range(2):
            arrived(bufs[q].at[k, y, x, core], send_z.at[q, k], recv_z.at[q, k], (tok, k))

    def place(q, a, b):
        return (b, a) if q == 0 else (a, b)

    sides = ((nx, ny), (ny, nx))
    mine_at = ((x, y), (y, x))

    def block(q, k, a, b):
        yy, xx = place(q, a, b)
        return bufs[q].at[k, yy, xx, core]

    def device(q, a, b):
        yy, xx = place(q, a, b)
        return (tok_of(yy, xx, core), voc)

    def second_axis(q, k, a, src):
        b = mine_at[q][1]
        for i in range(1, sides[q][1]):
            to = lax.rem(b + i, sides[q][1])
            push(src, block(q, k, a, b), send_b.at[q, k, to, a], recv_b.at[q, k, b, a],
                 device(q, mine_at[q][0], to))

    def first_hop(j):
        k = partner(voc, j, n_voc)
        for q in range(2):
            a, b = mine_at[q]
            for i in range(1, sides[q][0]):
                to = lax.rem(a + i, sides[q][0])
                push(srcs[q] if j == 0 else block(q, k, a, b), block(q, k, a, b),
                     send_a.at[q, k, to], recv_a.at[q, k, a], device(q, to, b))
        for q in range(2):
            a, b = mine_at[q]
            second_axis(q, k, a, srcs[q] if j == 0 else block(q, k, a, b))

    def second_hop(j):
        k = partner(voc, j, n_voc)
        for q in range(2):
            a, b = mine_at[q]
            for i in range(1, sides[q][0]):
                at = lax.rem(a + i, sides[q][0])
                arrived(block(q, k, at, b), send_a.at[q, k, at], recv_a.at[q, k, at],
                        device(q, at, b))
                second_axis(q, k, at, block(q, k, at, b))
        for q in range(2):
            to_other_core(q, k, mine_at[q][1])

    def across(q, k, b, cc):
        return bufs[q].at[k, b, :, cc] if q == 0 else bufs[q].at[k, :, b, cc]

    def to_other_core(q, k, b):
        for i in range(1, nc):
            to = lax.rem(core + i, nc)
            push(across(q, k, b, core), across(q, k, b, core),
                 send_c.at[q, k, b], recv_c.at[q, k, b], (tok_of(y, x, to), voc))

    def core_hop(j):
        k = partner(voc, j, n_voc)
        for q in range(2):
            a, b = mine_at[q]
            for i in range(1, sides[q][1]):
                at = lax.rem(b + i, sides[q][1])
                for n in range(sides[q][0]):
                    arrived(block(q, k, n, at), send_b.at[q, k, at, n], recv_b.at[q, k, at, n],
                            device(q, a, at))
                to_other_core(q, k, at)

    def wait_core(j):
        k = partner(voc, j, n_voc)
        for i in range(1, nc):
            cc = lax.rem(core + i, nc)
            for q in range(2):
                for n in range(sides[q][1]):
                    arrived(across(q, k, n, cc), send_c.at[q, k, n], recv_c.at[q, k, n],
                            (tok_of(y, x, cc), voc))

    def product(j):
        k = partner(voc, j, n_voc)
        out = []
        for buf, head in ((bt, vt), (bs, vs)):
            depth = buf.shape[-1]
            rows = buf[k].reshape(tokens, depth)
            part = head[pl.ds(pl.multiple_of(k * depth, depth), depth), :]
            out.append(jnp.dot(rows, part, preferred_element_type=F32))
        return out

    u = jnp.zeros((tokens, cols), F32)
    s = jnp.zeros((tokens, cols), F32)
    for j in range(n_voc + 3):
        if j == 0:
            if n_voc > 1:
                send_along_z(1)
            first_hop(0)
            for i in range(2, n_voc):
                send_along_z(i)
            for copy in own:
                copy.wait()
        elif j < n_voc:
            wait_along_z(j)
            first_hop(j)
        if 0 <= j - 1 < n_voc:
            second_hop(j - 1)
        if 0 <= j - 2 < n_voc:
            core_hop(j - 2)
        if 0 <= j - 3 < n_voc:
            wait_core(j - 3)
            du, ds = product(j - 3)
            u = u + du
            s = s + ds

    perm = (lax.broadcasted_iota(jnp.int32, (tokens, tokens), 0) == route[...]).astype(BF16)
    hi = u.astype(BF16)
    rest = u - hi.astype(F32)
    mid = rest.astype(BF16)
    low = (rest - mid.astype(F32)).astype(BF16)
    move = lambda part: jnp.dot(perm, part, preferred_element_type=F32)
    u = (move(hi) + move(mid)) + move(low)
    s, u = s.T, u.T

    entry = lax.broadcasted_iota(jnp.int32, (cols, tokens), 0) + first_col
    picked = entry == ids[...]
    ms = jnp.max(s, axis=0, keepdims=True)
    mu = jnp.max(u, axis=0, keepdims=True)
    cs, cu = s - ms, u - mu
    es = jnp.exp(cs)
    total = lambda a: jnp.sum(a, axis=0, keepdims=True)
    mine = (
        ms, total(es), mu, total(jnp.exp(cu)), total(es * (cs - cu)),
        total(jnp.where(picked, s, 0.0)), total(jnp.where(picked, u, 0.0)),
    )

    def put(slots, at, values):
        for q, value in enumerate(values):
            slots[at, q:q + 1, :] = value
        slots[at, 7:8, :] = jnp.zeros_like(values[0])

    put(stat1, tok, mine)
    for i in range(1, n_tok):
        to = lax.rem(tok + i, n_tok)
        push(stat1.at[tok], stat1.at[tok], send_1.at[to], recv_1.at[tok], (to, voc))

    for k in range(n_voc):
        rows_t_out[k] = bs[k].reshape(tokens, hs.shape[1]).T

    for i in range(1, n_tok):
        at = lax.rem(tok + i, n_tok)
        arrived(stat1.at[at], send_1.at[at], recv_1.at[at], (at, voc))
    put(stat2, voc, merge(stat1[...]))
    for j in range(1, n_voc):
        to = partner(voc, j, n_voc)
        push(stat2.at[voc], stat2.at[voc], send_2.at[to], recv_2.at[voc], (tok, to))
    position = lax.broadcasted_iota(jnp.int32, (1, tokens), 1)
    limit = jnp.zeros((1, tokens), jnp.int32)
    for w in range(n_tok):
        limit = jnp.where(position // grp == w, lengths[w], limit)
    live = (lax.rem(position, grp) < limit).astype(F32)
    for j in range(1, n_voc):
        at = partner(voc, j, n_voc)
        arrived(stat2.at[at], send_2.at[at], recv_2.at[at], (tok, at))
    ms, zs, mu, zu, acc, ps, pu = merge(stat2[...])
    log_zs, log_zu = jnp.log(zs), jnp.log(zu)
    kl = acc / zs - log_zs + log_zu
    mixed = 1.0 / (0.2 * jnp.exp((pu - mu - log_zu) - (ps - ms - log_zs)) + 0.8)
    weight = jnp.where(flags[...] == 1, mixed, 1.0)
    ls = s - ms - log_zs
    gap = ls - (u - mu - log_zu)
    dl = (live * weight) * jnp.exp(ls) * (gap - kl)
    dl_out[...] = dl.T.astype(BF16)
    div_out[...] = live * kl
    for copy in started:
        copy.wait_send()


def grad_kernel(n_tok, rows_t, dl, div_all, grad, div, made, sems):
    n_voc, fs, tokens = rows_t.shape
    copies = []
    for k in range(n_voc):
        made[k] = jnp.dot(rows_t[k], dl[...], preferred_element_type=F32).astype(BF16)
        copies.append(pltpu.make_async_copy(made.at[k], grad.at[pl.ds(k * fs, fs)], sems.at[k]))
        copies[-1].start()
    grp = tokens // n_tok
    shift = lax.rem(tokens - lax.axis_index("tok") * grp, tokens)
    turned = pltpu.roll(jnp.broadcast_to(div_all[...], (8, tokens)), shift, 1)
    div[...] = turned[0:1, :grp]
    for copy in copies:
        copy.wait()


def on_device(
    n_tok, n_voc, student_hidden, teacher_rows, student_head, teacher_head,
    lengths, route, sampled_ids, mix_flags,
):
    grp, fs = student_hidden.shape
    ft = teacher_rows.shape[1]
    tokens = grp * n_tok
    ds, cols = student_head.shape
    dt = teacher_head.shape[0]
    ny, nx, nc = grid_of(n_tok)
    side = max(nx, ny)
    dma = pltpu.SemaphoreType.DMA
    hbm = pl.BlockSpec(memory_space=pltpu.HBM)
    vmem = pl.BlockSpec(memory_space=pltpu.VMEM)
    line = lambda a: a.reshape(1, tokens)
    rows_t, dl, div_all = pl.pallas_call(
        functools.partial(gather_kernel, n_tok, n_voc),
        out_shape=(
            jax.ShapeDtypeStruct((n_voc, fs, tokens), BF16),
            jax.ShapeDtypeStruct((tokens, cols), BF16),
            jax.ShapeDtypeStruct((1, tokens), F32),
        ),
        in_specs=[hbm] * 8,
        out_specs=(vmem, vmem, vmem),
        scratch_shapes=[
            pltpu.SMEM(lengths.shape, jnp.int32),
            pltpu.VMEM((1, tokens), jnp.int32),
            pltpu.VMEM((1, tokens), jnp.int32),
            pltpu.VMEM((1, tokens), jnp.int32),
            pltpu.VMEM((n_voc, ny, nx, nc, grp, fs), BF16),
            pltpu.VMEM((n_voc, ny, nx, nc, grp, ft), BF16),
            pltpu.VMEM((ds, cols), BF16),
            pltpu.VMEM((dt, cols), BF16),
            pltpu.VMEM((n_tok, 8, tokens), F32),
            pltpu.VMEM((n_voc, 8, tokens), F32),
            dma((2, n_voc)), dma((2, n_voc)),
            dma((2, n_voc, side)), dma((2, n_voc, side)),
            dma((2, n_voc, side, side)), dma((2, n_voc, side, side)),
            dma((2, n_voc, side)), dma((2, n_voc, side)),
            dma((n_tok,)), dma((n_tok,)),
            dma((n_voc,)), dma((n_voc,)),
            dma((8,)),
        ],
        compiler_params=pltpu.CompilerParams(
            collective_id=0, has_side_effects=True, vmem_limit_bytes=40 << 20
        ),
        name="gather_and_softmax",
    )(
        *[pltpu.with_memory_space_constraint(a, pltpu.HBM) for a in (
            student_hidden, teacher_rows, student_head, teacher_head,
            lengths, line(route), line(sampled_ids), line(mix_flags),
        )]
    )
    grad, div = pl.pallas_call(
        functools.partial(grad_kernel, n_tok),
        out_shape=(
            jax.ShapeDtypeStruct((ds, cols), BF16),
            jax.ShapeDtypeStruct((1, grp), F32),
        ),
        in_specs=[vmem] * 3,
        out_specs=(hbm, vmem),
        scratch_shapes=[pltpu.VMEM((n_voc, fs, cols), BF16), dma((n_voc,))],
        compiler_params=pltpu.CompilerParams(vmem_limit_bytes=12 << 20),
        name="head_grad",
    )(rows_t, dl, div_all)
    return div.reshape(grp), grad


def solution(mesh):
    in_specs = (
        P("tok", "voc"),
        P("tok", "voc"),
        P(None, ("tok", "voc")),
        P(None, ("tok", "voc")),
        P(),
        P(),
        P(),
        P(),
    )
    out_specs = (P("tok"), P(None, ("tok", "voc")))
    body = functools.partial(on_device, mesh.shape["tok"], mesh.shape["voc"])
    return jax.shard_map(body, mesh=mesh, in_specs=in_specs, out_specs=out_specs, check_vma=False)
```

```python
import functools
import math

import jax
import jax.numpy as jnp
from jax import lax
from jax.experimental import pallas as pl
from jax.experimental.pallas import tpu as pltpu
from jax.sharding import PartitionSpec as P

MESH = pl.DeviceIdType.MESH
F32 = jnp.float32
BF16 = jnp.bfloat16


def grid_of(n_tok):
    cores = 2 if n_tok % 2 == 0 else 1
    chips = n_tok // cores
    wide = math.isqrt(chips)
    while chips % wide:
        wide -= 1
    return chips // wide, wide, cores


def partner(me, step, count):
    if count & (count - 1):
        return lax.rem(me + step, count)
    out = me
    bit = 1
    while bit < count:
        if step & bit:
            out = out + bit - 2 * bit * lax.rem(out // bit, 2)
        bit *= 2
    return out


def merge(block):
    row = lambda q: block[:, q:q + 1, :]
    ms, zs, mu, zu, acc, ps, pu = [row(q) for q in range(7)]
    top_s, top_u = jnp.max(ms, axis=0), jnp.max(mu, axis=0)
    ds, du = ms - top_s[None], mu - top_u[None]
    es = jnp.exp(ds)
    return (
        top_s,
        jnp.sum(zs * es, axis=0),
        top_u,
        jnp.sum(zu * jnp.exp(du), axis=0),
        jnp.sum(es * (acc + zs * (ds - du)), axis=0),
        jnp.sum(ps, axis=0),
        jnp.sum(pu, axis=0),
    )


def gather_kernel(
    n_tok, n_voc, hs, ht, ws, wt, lengths_in, route_in, ids_in, flags_in,
    rows_t_out, dl_out, div_out,
    lengths, route, ids, flags, bs, bt, vs, vt, stat1, stat2,
    send_z, recv_z, send_a, recv_a, send_b, recv_b, send_c, recv_c,
    send_1, recv_1, send_2, recv_2, loc,
):
    ny, nx, nc = grid_of(n_tok)
    tok, voc = lax.axis_index("tok"), lax.axis_index("voc")
    core = lax.rem(tok, nc)
    x = lax.rem(tok // nc, nx)
    y = tok // (nc * nx)
    tok_of = lambda yy, xx, cc: (yy * nx + xx) * nc + cc
    grp = hs.shape[0]
    tokens = grp * n_tok
    cols = ws.shape[1]
    first_col = (tok * n_voc + voc) * cols

    own = [
        pltpu.make_async_copy(hs, bs.at[voc, y, x, core], loc.at[0]),
        pltpu.make_async_copy(ht, bt.at[voc, y, x, core], loc.at[1]),
        pltpu.make_async_copy(ws, vs, loc.at[2]),
        pltpu.make_async_copy(wt, vt, loc.at[3]),
        pltpu.make_async_copy(lengths_in, lengths, loc.at[4]),
        pltpu.make_async_copy(route_in, route, loc.at[5]),
        pltpu.make_async_copy(ids_in, ids, loc.at[6]),
        pltpu.make_async_copy(flags_in, flags, loc.at[7]),
    ]
    for copy in own:
        copy.start()

    barrier = pltpu.get_barrier_semaphore()
    for i in range(1, n_tok):
        pl.semaphore_signal(
            barrier, inc=1, device_id=(lax.rem(tok + i, n_tok), voc), device_id_type=MESH
        )
    for j in range(1, n_voc):
        pl.semaphore_signal(
            barrier, inc=1, device_id=(tok, partner(voc, j, n_voc)), device_id_type=MESH
        )
    pl.semaphore_wait(barrier, n_tok + n_voc - 2)

    started = []

    def push(src, dst, ssem, rsem, device):
        copy = pltpu.make_async_remote_copy(
            src_ref=src, dst_ref=dst, send_sem=ssem, recv_sem=rsem,
            device_id=device, device_id_type=MESH,
        )
        copy.start()
        started.append(copy)

    def arrived(dst, ssem, rsem, device):
        pltpu.make_async_remote_copy(
            src_ref=dst, dst_ref=dst, send_sem=ssem, recv_sem=rsem,
            device_id=device, device_id_type=MESH,
        ).wait_recv()

    bufs = (bt, bs)
    srcs = (ht, hs)

    def send_along_z(j):
        to = partner(voc, j, n_voc)
        for q in range(2):
            push(srcs[q], bufs[q].at[voc, y, x, core],
                 send_z.at[q, to], recv_z.at[q, voc], (tok, to))

    def wait_along_z(j):
        k = partner(voc, j, n_voc)
        for q in range(2):
            arrived(bufs[q].at[k, y, x, core], send_z.at[q, k], recv_z.at[q, k], (tok, k))

    sides = ((nx, ny), (ny, nx))
    mine_at = ((x, y), (y, x))
    turn = lambda q, j: (q + j) % 2

    def place(o, a, b):
        return (b, a) if o == 0 else (a, b)

    def block(q, o, k, a, b):
        yy, xx = place(o, a, b)
        return bufs[q].at[k, yy, xx, core]

    def device(o, a, b):
        yy, xx = place(o, a, b)
        return (tok_of(yy, xx, core), voc)

    def second_axis(q, o, k, a, src):
        b = mine_at[o][1]
        for i in range(1, sides[o][1]):
            to = lax.rem(b + i, sides[o][1])
            push(src, block(q, o, k, a, b), send_b.at[q, k, to, a], recv_b.at[q, k, b, a],
                 device(o, mine_at[o][0], to))

    def first_hop(j):
        k = partner(voc, j, n_voc)
        for q in range(2):
            o = turn(q, j)
            a, b = mine_at[o]
            for i in range(1, sides[o][0]):
                to = lax.rem(a + i, sides[o][0])
                push(srcs[q] if j == 0 else block(q, o, k, a, b), block(q, o, k, a, b),
                     send_a.at[q, k, to], recv_a.at[q, k, a], device(o, to, b))
        for q in range(2):
            o = turn(q, j)
            a, b = mine_at[o]
            second_axis(q, o, k, a, srcs[q] if j == 0 else block(q, o, k, a, b))

    def second_hop(j):
        k = partner(voc, j, n_voc)
        for q in range(2):
            o = turn(q, j)
            a, b = mine_at[o]
            for i in range(1, sides[o][0]):
                at = lax.rem(a + i, sides[o][0])
                arrived(block(q, o, k, at, b), send_a.at[q, k, at], recv_a.at[q, k, at],
                        device(o, at, b))
                second_axis(q, o, k, at, block(q, o, k, at, b))
        if j == 0:
            for copy in own[:2]:
                copy.wait()
        for q in range(2):
            o = turn(q, j)
            to_other_core(q, o, k, mine_at[o][1])

    def across(q, o, k, b, cc):
        return bufs[q].at[k, b, :, cc] if o == 0 else bufs[q].at[k, :, b, cc]

    def to_other_core(q, o, k, b):
        for i in range(1, nc):
            to = lax.rem(core + i, nc)
            push(across(q, o, k, b, core), across(q, o, k, b, core),
                 send_c.at[q, k, b], recv_c.at[q, k, b], (tok_of(y, x, to), voc))

    def core_hop(j):
        k = partner(voc, j, n_voc)
        for q in range(2):
            o = turn(q, j)
            a, b = mine_at[o]
            for i in range(1, sides[o][1]):
                at = lax.rem(b + i, sides[o][1])
                for n in range(sides[o][0]):
                    arrived(block(q, o, k, n, at), send_b.at[q, k, at, n], recv_b.at[q, k, at, n],
                            device(o, a, at))
                to_other_core(q, o, k, at)

    def wait_core(j):
        k = partner(voc, j, n_voc)
        for i in range(1, nc):
            cc = lax.rem(core + i, nc)
            for q in range(2):
                o = turn(q, j)
                for n in range(sides[o][1]):
                    arrived(across(q, o, k, n, cc), send_c.at[q, k, n], recv_c.at[q, k, n],
                            (tok_of(y, x, cc), voc))

    def product(j):
        k = partner(voc, j, n_voc)
        out = []
        for buf, head in ((bt, vt), (bs, vs)):
            depth = buf.shape[-1]
            rows = buf[k].reshape(tokens, depth)
            part = head[pl.ds(pl.multiple_of(k * depth, depth), depth), :]
            out.append(jnp.dot(rows, part, preferred_element_type=F32))
        return out

    def features_first(j):
        k = partner(voc, j, n_voc)
        rows_t_out[k] = bs[k].reshape(tokens, hs.shape[1]).T

    u = jnp.zeros((tokens, cols), F32)
    s = jnp.zeros((tokens, cols), F32)
    for j in range(n_voc + 3):
        if j == 0:
            if n_voc > 1:
                send_along_z(1)
            first_hop(0)
            for i in range(2, n_voc):
                send_along_z(i)
        elif j < n_voc:
            wait_along_z(j)
            first_hop(j)
        if 0 <= j - 1 < n_voc:
            second_hop(j - 1)
        if 0 <= j - 2 < n_voc:
            core_hop(j - 2)
        if 0 <= j - 3 < n_voc:
            wait_core(j - 3)
            if j == 3:
                for copy in own[2:]:
                    copy.wait()
            du, ds = product(j - 3)
            u = u + du
            s = s + ds
            if j - 3 < n_voc - 1:
                features_first(j - 3)

    perm = (lax.broadcasted_iota(jnp.int32, (tokens, tokens), 0) == route[...]).astype(BF16)
    hi = u.astype(BF16)
    rest = u - hi.astype(F32)
    mid = rest.astype(BF16)
    low = (rest - mid.astype(F32)).astype(BF16)
    move = lambda part: jnp.dot(perm, part, preferred_element_type=F32)
    u = (move(hi) + move(mid)) + move(low)
    s, u = s.T, u.T

    entry = lax.broadcasted_iota(jnp.int32, (cols, tokens), 0) + first_col
    picked = entry == ids[...]
    ms = jnp.max(s, axis=0, keepdims=True)
    mu = jnp.max(u, axis=0, keepdims=True)
    cs, cu = s - ms, u - mu
    es = jnp.exp(cs)
    total = lambda a: jnp.sum(a, axis=0, keepdims=True)
    mine = (
        ms, total(es), mu, total(jnp.exp(cu)), total(es * (cs - cu)),
        total(jnp.where(picked, s, 0.0)), total(jnp.where(picked, u, 0.0)),
    )

    def put(slots, at, values):
        for q, value in enumerate(values):
            slots[at, q:q + 1, :] = value
        slots[at, 7:8, :] = jnp.zeros_like(values[0])

    put(stat1, tok, mine)
    for i in range(1, n_tok):
        to = lax.rem(tok + i, n_tok)
        push(stat1.at[tok], stat1.at[tok], send_1.at[to], recv_1.at[tok], (to, voc))

    features_first(n_voc - 1)

    for i in range(1, n_tok):
        at = lax.rem(tok + i, n_tok)
        arrived(stat1.at[at], send_1.at[at], recv_1.at[at], (at, voc))
    put(stat2, voc, merge(stat1[...]))
    for j in range(1, n_voc):
        to = partner(voc, j, n_voc)
        push(stat2.at[voc], stat2.at[voc], send_2.at[to], recv_2.at[voc], (tok, to))
    position = lax.broadcasted_iota(jnp.int32, (1, tokens), 1)
    limit = jnp.zeros((1, tokens), jnp.int32)
    for w in range(n_tok):
        limit = jnp.where(position // grp == w, lengths[w], limit)
    live = (lax.rem(position, grp) < limit).astype(F32)
    for j in range(1, n_voc):
        at = partner(voc, j, n_voc)
        arrived(stat2.at[at], send_2.at[at], recv_2.at[at], (tok, at))
    ms, zs, mu, zu, acc, ps, pu = merge(stat2[...])
    log_zs, log_zu = jnp.log(zs), jnp.log(zu)
    kl = acc / zs - log_zs + log_zu
    mixed = 1.0 / (0.2 * jnp.exp((pu - mu - log_zu) - (ps - ms - log_zs)) + 0.8)
    weight = jnp.where(flags[...] == 1, mixed, 1.0)
    ls = s - ms - log_zs
    gap = ls - (u - mu - log_zu)
    dl = (live * weight) * jnp.exp(ls) * (gap - kl)
    dl_out[...] = dl.T.astype(BF16)
    div_out[...] = live * kl
    for copy in started:
        copy.wait_send()


def grad_kernel(n_tok, rows_t, dl, div_all, grad, div, made, sems):
    n_voc, fs, tokens = rows_t.shape
    copies = []
    for k in range(n_voc):
        made[k] = jnp.dot(rows_t[k], dl[...], preferred_element_type=F32).astype(BF16)
        copies.append(pltpu.make_async_copy(made.at[k], grad.at[pl.ds(k * fs, fs)], sems.at[k]))
        copies[-1].start()
    grp = tokens // n_tok
    shift = lax.rem(tokens - lax.axis_index("tok") * grp, tokens)
    turned = pltpu.roll(jnp.broadcast_to(div_all[...], (8, tokens)), shift, 1)
    div[...] = turned[0:1, :grp]
    for copy in copies:
        copy.wait()


def on_device(
    n_tok, n_voc, student_hidden, teacher_rows, student_head, teacher_head,
    lengths, route, sampled_ids, mix_flags,
):
    grp, fs = student_hidden.shape
    ft = teacher_rows.shape[1]
    tokens = grp * n_tok
    ds, cols = student_head.shape
    dt = teacher_head.shape[0]
    ny, nx, nc = grid_of(n_tok)
    side = max(nx, ny)
    dma = pltpu.SemaphoreType.DMA
    hbm = pl.BlockSpec(memory_space=pltpu.HBM)
    vmem = pl.BlockSpec(memory_space=pltpu.VMEM)
    line = lambda a: a.reshape(1, tokens)
    rows_t, dl, div_all = pl.pallas_call(
        functools.partial(gather_kernel, n_tok, n_voc),
        out_shape=(
            jax.ShapeDtypeStruct((n_voc, fs, tokens), BF16),
            jax.ShapeDtypeStruct((tokens, cols), BF16),
            jax.ShapeDtypeStruct((1, tokens), F32),
        ),
        in_specs=[hbm] * 8,
        out_specs=(vmem, vmem, vmem),
        scratch_shapes=[
            pltpu.SMEM(lengths.shape, jnp.int32),
            pltpu.VMEM((1, tokens), jnp.int32),
            pltpu.VMEM((1, tokens), jnp.int32),
            pltpu.VMEM((1, tokens), jnp.int32),
            pltpu.VMEM((n_voc, ny, nx, nc, grp, fs), BF16),
            pltpu.VMEM((n_voc, ny, nx, nc, grp, ft), BF16),
            pltpu.VMEM((ds, cols), BF16),
            pltpu.VMEM((dt, cols), BF16),
            pltpu.VMEM((n_tok, 8, tokens), F32),
            pltpu.VMEM((n_voc, 8, tokens), F32),
            dma((2, n_voc)), dma((2, n_voc)),
            dma((2, n_voc, side)), dma((2, n_voc, side)),
            dma((2, n_voc, side, side)), dma((2, n_voc, side, side)),
            dma((2, n_voc, side)), dma((2, n_voc, side)),
            dma((n_tok,)), dma((n_tok,)),
            dma((n_voc,)), dma((n_voc,)),
            dma((8,)),
        ],
        compiler_params=pltpu.CompilerParams(
            collective_id=0, has_side_effects=True, vmem_limit_bytes=40 << 20
        ),
        name="gather_and_softmax",
    )(
        *[pltpu.with_memory_space_constraint(a, pltpu.HBM) for a in (
            student_hidden, teacher_rows, student_head, teacher_head,
            lengths, line(route), line(sampled_ids), line(mix_flags),
        )]
    )
    grad, div = pl.pallas_call(
        functools.partial(grad_kernel, n_tok),
        out_shape=(
            jax.ShapeDtypeStruct((ds, cols), BF16),
            jax.ShapeDtypeStruct((1, grp), F32),
        ),
        in_specs=[vmem] * 3,
        out_specs=(hbm, vmem),
        scratch_shapes=[pltpu.VMEM((n_voc, fs, cols), BF16), dma((n_voc,))],
        compiler_params=pltpu.CompilerParams(vmem_limit_bytes=12 << 20),
        name="head_grad",
    )(rows_t, dl, div_all)
    return div.reshape(grp), grad


def solution(mesh):
    in_specs = (
        P("tok", "voc"),
        P("tok", "voc"),
        P(None, ("tok", "voc")),
        P(None, ("tok", "voc")),
        P(),
        P(),
        P(),
        P(),
    )
    out_specs = (P("tok"), P(None, ("tok", "voc")))
    body = functools.partial(on_device, mesh.shape["tok"], mesh.shape["voc"])
    return jax.shard_map(body, mesh=mesh, in_specs=in_specs, out_specs=out_specs, check_vma=False)
```

```python
import functools
import math

import jax
import jax.numpy as jnp
from jax import lax
from jax.experimental import pallas as pl
from jax.experimental.pallas import tpu as pltpu
from jax.sharding import PartitionSpec as P

MESH = pl.DeviceIdType.MESH
F32 = jnp.float32
BF16 = jnp.bfloat16


def grid_of(n_tok):
    cores = 2 if n_tok % 2 == 0 else 1
    chips = n_tok // cores
    wide = math.isqrt(chips)
    while chips % wide:
        wide -= 1
    return chips // wide, wide, cores


def partner(me, step, count):
    if count & (count - 1):
        return lax.rem(me + step, count)
    out = me
    bit = 1
    while bit < count:
        if step & bit:
            out = out + bit - 2 * bit * lax.rem(out // bit, 2)
        bit *= 2
    return out


def merge(block):
    row = lambda q: block[:, q:q + 1, :]
    ms, zs, mu, zu, acc, ps, pu = [row(q) for q in range(7)]
    top_s, top_u = jnp.max(ms, axis=0), jnp.max(mu, axis=0)
    ds, du = ms - top_s[None], mu - top_u[None]
    es = jnp.exp(ds)
    return (
        top_s,
        jnp.sum(zs * es, axis=0),
        top_u,
        jnp.sum(zu * jnp.exp(du), axis=0),
        jnp.sum(es * (acc + zs * (ds - du)), axis=0),
        jnp.sum(ps, axis=0),
        jnp.sum(pu, axis=0),
    )


def gather_kernel(
    n_tok, n_voc, hs, ht, ws, wt, lengths_in, route_in, ids_in, flags_in,
    rows_t_out, dl_out, div_out,
    lengths, route, ids, flags, buf, hs_v, ht_v, vs, vt, stat1, stat2,
    send_z, recv_z, send_a, recv_a, send_b, recv_b, send_d, send_c, recv_c,
    send_1, recv_1, send_2, recv_2, loc,
):
    ny, nx, nc = grid_of(n_tok)
    tok, voc = lax.axis_index("tok"), lax.axis_index("voc")
    core = lax.rem(tok, nc)
    x = lax.rem(tok // nc, nx)
    y = tok // (nc * nx)
    tok_of = lambda yy, xx, cc: (yy * nx + xx) * nc + cc
    grp = hs.shape[0]
    tokens = grp * n_tok
    cols = ws.shape[1]
    fs, ft = hs.shape[1], ht.shape[1]
    first_col = (tok * n_voc + voc) * cols

    own = [
        pltpu.make_async_copy(hs, hs_v, loc.at[0]),
        pltpu.make_async_copy(ht, ht_v, loc.at[1]),
        pltpu.make_async_copy(ws, vs, loc.at[2]),
        pltpu.make_async_copy(wt, vt, loc.at[3]),
        pltpu.make_async_copy(lengths_in, lengths, loc.at[4]),
        pltpu.make_async_copy(route_in, route, loc.at[5]),
        pltpu.make_async_copy(ids_in, ids, loc.at[6]),
        pltpu.make_async_copy(flags_in, flags, loc.at[7]),
    ]
    for copy in own:
        copy.start()

    barrier = pltpu.get_barrier_semaphore()
    for i in range(1, n_tok):
        pl.semaphore_signal(
            barrier, inc=1, device_id=(lax.rem(tok + i, n_tok), voc), device_id_type=MESH
        )
    for j in range(1, n_voc):
        pl.semaphore_signal(
            barrier, inc=1, device_id=(tok, partner(voc, j, n_voc)), device_id_type=MESH
        )
    for copy in own[:2]:
        copy.wait()
    buf[voc, y, x, core, :, :ft] = ht_v[...]
    buf[voc, y, x, core, :, ft:] = hs_v[...]
    pl.semaphore_wait(barrier, n_tok + n_voc - 2)

    started = []

    def push(src, dst, ssem, rsem, device):
        copy = pltpu.make_async_remote_copy(
            src_ref=src, dst_ref=dst, send_sem=ssem, recv_sem=rsem,
            device_id=device, device_id_type=MESH,
        )
        copy.start()
        started.append(copy)

    def arrived(dst, ssem, rsem, device):
        pltpu.make_async_remote_copy(
            src_ref=dst, dst_ref=dst, send_sem=ssem, recv_sem=rsem,
            device_id=device, device_id_type=MESH,
        ).wait_recv()

    def send_along_z(j):
        to = partner(voc, j, n_voc)
        block = buf.at[voc, y, x, core]
        push(block, block, send_z.at[to], recv_z.at[voc], (tok, to))

    def wait_along_z(j):
        k = partner(voc, j, n_voc)
        arrived(buf.at[k, y, x, core], send_z.at[k], recv_z.at[k], (tok, k))

    sides = ((nx, ny), (ny, nx))
    mine_at = ((x, y), (y, x))
    direct = lambda j: j == n_voc - 1

    def place(o, a, b):
        return (b, a) if o == 0 else (a, b)

    def block_at(o, k, a, b):
        yy, xx = place(o, a, b)
        return buf.at[k, yy, xx, core]

    def device(o, a, b):
        yy, xx = place(o, a, b)
        return (tok_of(yy, xx, core), voc)

    def second_axis(o, k, a):
        b = mine_at[o][1]
        for i in range(1, sides[o][1]):
            to = lax.rem(b + i, sides[o][1])
            push(block_at(o, k, a, b), block_at(o, k, a, b), send_b.at[k, to, a],
                 recv_b.at[k, b, a], device(o, mine_at[o][0], to))

    def first_hop(j):
        k, o = partner(voc, j, n_voc), j % 2
        a, b = mine_at[o]
        block = block_at(o, k, a, b)
        if direct(j):
            for i in range(1, sides[o][0]):
                for n in range(1, sides[o][1]):
                    to_a, to_b = lax.rem(a + i, sides[o][0]), lax.rem(b + n, sides[o][1])
                    push(block, block, send_d.at[to_a, to_b], recv_b.at[k, b, a],
                         device(o, to_a, to_b))
        for i in range(1, sides[o][0]):
            to = lax.rem(a + i, sides[o][0])
            push(block, block, send_a.at[k, to], recv_a.at[k, a], device(o, to, b))
        second_axis(o, k, a)

    def second_hop(j):
        k, o = partner(voc, j, n_voc), j % 2
        a, b = mine_at[o]
        for i in range(1, sides[o][0]):
            at = lax.rem(a + i, sides[o][0])
            arrived(block_at(o, k, at, b), send_a.at[k, at], recv_a.at[k, at], device(o, at, b))
            if not direct(j):
                second_axis(o, k, at)

    def core_hop(j):
        k, o = partner(voc, j, n_voc), j % 2
        a, b = mine_at[o]
        for i in range(1, sides[o][1]):
            at = lax.rem(b + i, sides[o][1])
            for n in range(sides[o][0]):
                arrived(block_at(o, k, n, at), send_b.at[k, at, n], recv_b.at[k, at, n],
                        device(o, a, at))
        for i in range(1, nc):
            to = lax.rem(core + i, nc)
            push(buf.at[k, :, :, core], buf.at[k, :, :, core],
                 send_c.at[k], recv_c.at[k], (tok_of(y, x, to), voc))

    def wait_core(j):
        k = partner(voc, j, n_voc)
        for i in range(1, nc):
            cc = lax.rem(core + i, nc)
            arrived(buf.at[k, :, :, cc], send_c.at[k], recv_c.at[k], (tok_of(y, x, cc), voc))

    def product(j):
        k = partner(voc, j, n_voc)
        out = []
        for first, depth, head in ((0, ft, vt), (ft, fs, vs)):
            rows = buf[k, :, :, :, :, first:first + depth].reshape(tokens, depth)
            part = head[pl.ds(pl.multiple_of(k * depth, depth), depth), :]
            out.append(jnp.dot(rows, part, preferred_element_type=F32))
        return out

    def features_first(j):
        k = partner(voc, j, n_voc)
        rows_t_out[k] = buf[k, :, :, :, :, ft:].reshape(tokens, fs).T

    u = jnp.zeros((tokens, cols), F32)
    s = jnp.zeros((tokens, cols), F32)
    for j in range(n_voc + 3):
        if j == 0:
            if n_voc > 1:
                send_along_z(1)
            first_hop(0)
            for i in range(2, n_voc):
                send_along_z(i)
        elif j < n_voc:
            wait_along_z(j)
            first_hop(j)
        if 0 <= j - 1 < n_voc:
            second_hop(j - 1)
        if 0 <= j - 2 < n_voc:
            core_hop(j - 2)
        if 0 <= j - 3 < n_voc:
            wait_core(j - 3)
            if j == 3:
                for copy in own[2:]:
                    copy.wait()
            du, ds = product(j - 3)
            u = u + du
            s = s + ds
            if j - 3 < n_voc - 1:
                features_first(j - 3)

    perm = (lax.broadcasted_iota(jnp.int32, (tokens, tokens), 0) == route[...]).astype(BF16)
    hi = u.astype(BF16)
    rest = u - hi.astype(F32)
    mid = rest.astype(BF16)
    low = (rest - mid.astype(F32)).astype(BF16)
    move = lambda part: jnp.dot(perm, part, preferred_element_type=F32)
    u = (move(hi) + move(mid)) + move(low)
    s, u = s.T, u.T

    entry = lax.broadcasted_iota(jnp.int32, (cols, tokens), 0) + first_col
    picked = entry == ids[...]
    ms = jnp.max(s, axis=0, keepdims=True)
    mu = jnp.max(u, axis=0, keepdims=True)
    cs, cu = s - ms, u - mu
    es = jnp.exp(cs)
    total = lambda a: jnp.sum(a, axis=0, keepdims=True)
    mine = (
        ms, total(es), mu, total(jnp.exp(cu)), total(es * (cs - cu)),
        total(jnp.where(picked, s, 0.0)), total(jnp.where(picked, u, 0.0)),
    )

    def put(slots, at, values):
        for q, value in enumerate(values):
            slots[at, q:q + 1, :] = value
        slots[at, 7:8, :] = jnp.zeros_like(values[0])

    put(stat1, tok, mine)
    for i in range(1, n_tok):
        to = lax.rem(tok + i, n_tok)
        push(stat1.at[tok], stat1.at[tok], send_1.at[to], recv_1.at[tok], (to, voc))

    features_first(n_voc - 1)

    for i in range(1, n_tok):
        at = lax.rem(tok + i, n_tok)
        arrived(stat1.at[at], send_1.at[at], recv_1.at[at], (at, voc))
    put(stat2, voc, merge(stat1[...]))
    for j in range(1, n_voc):
        to = partner(voc, j, n_voc)
        push(stat2.at[voc], stat2.at[voc], send_2.at[to], recv_2.at[voc], (tok, to))
    position = lax.broadcasted_iota(jnp.int32, (1, tokens), 1)
    limit = jnp.zeros((1, tokens), jnp.int32)
    for w in range(n_tok):
        limit = jnp.where(position // grp == w, lengths[w], limit)
    live = (lax.rem(position, grp) < limit).astype(F32)
    for j in range(1, n_voc):
        at = partner(voc, j, n_voc)
        arrived(stat2.at[at], send_2.at[at], recv_2.at[at], (tok, at))
    ms, zs, mu, zu, acc, ps, pu = merge(stat2[...])
    log_zs, log_zu = jnp.log(zs), jnp.log(zu)
    kl = acc / zs - log_zs + log_zu
    mixed = 1.0 / (0.2 * jnp.exp((pu - mu - log_zu) - (ps - ms - log_zs)) + 0.8)
    weight = jnp.where(flags[...] == 1, mixed, 1.0)
    ls = s - ms - log_zs
    gap = ls - (u - mu - log_zu)
    dl = (live * weight) * jnp.exp(ls) * (gap - kl)
    dl_out[...] = dl.T.astype(BF16)
    div_out[...] = live * kl
    for copy in started:
        copy.wait_send()


def grad_kernel(n_tok, rows_t, dl, div_all, grad, div, made, sems):
    n_voc, fs, tokens = rows_t.shape
    copies = []
    for k in range(n_voc):
        made[k] = jnp.dot(rows_t[k], dl[...], preferred_element_type=F32).astype(BF16)
        copies.append(pltpu.make_async_copy(made.at[k], grad.at[pl.ds(k * fs, fs)], sems.at[k]))
        copies[-1].start()
    grp = tokens // n_tok
    shift = lax.rem(tokens - lax.axis_index("tok") * grp, tokens)
    turned = pltpu.roll(jnp.broadcast_to(div_all[...], (8, tokens)), shift, 1)
    div[...] = turned[0:1, :grp]
    for copy in copies:
        copy.wait()


def on_device(
    n_tok, n_voc, student_hidden, teacher_rows, student_head, teacher_head,
    lengths, route, sampled_ids, mix_flags,
):
    grp, fs = student_hidden.shape
    ft = teacher_rows.shape[1]
    tokens = grp * n_tok
    ds, cols = student_head.shape
    dt = teacher_head.shape[0]
    ny, nx, nc = grid_of(n_tok)
    side = max(nx, ny)
    dma = pltpu.SemaphoreType.DMA
    hbm = pl.BlockSpec(memory_space=pltpu.HBM)
    vmem = pl.BlockSpec(memory_space=pltpu.VMEM)
    line = lambda a: a.reshape(1, tokens)
    rows_t, dl, div_all = pl.pallas_call(
        functools.partial(gather_kernel, n_tok, n_voc),
        out_shape=(
            jax.ShapeDtypeStruct((n_voc, fs, tokens), BF16),
            jax.ShapeDtypeStruct((tokens, cols), BF16),
            jax.ShapeDtypeStruct((1, tokens), F32),
        ),
        in_specs=[hbm] * 8,
        out_specs=(vmem, vmem, vmem),
        scratch_shapes=[
            pltpu.SMEM(lengths.shape, jnp.int32),
            pltpu.VMEM((1, tokens), jnp.int32),
            pltpu.VMEM((1, tokens), jnp.int32),
            pltpu.VMEM((1, tokens), jnp.int32),
            pltpu.VMEM((n_voc, ny, nx, nc, grp, ft + fs), BF16),
            pltpu.VMEM((grp, fs), BF16),
            pltpu.VMEM((grp, ft), BF16),
            pltpu.VMEM((ds, cols), BF16),
            pltpu.VMEM((dt, cols), BF16),
            pltpu.VMEM((n_tok, 8, tokens), F32),
            pltpu.VMEM((n_voc, 8, tokens), F32),
            dma((n_voc,)), dma((n_voc,)),
            dma((n_voc, side)), dma((n_voc, side)),
            dma((n_voc, side, side)), dma((n_voc, side, side)),
            dma((side, side)),
            dma((n_voc,)), dma((n_voc,)),
            dma((n_tok,)), dma((n_tok,)),
            dma((n_voc,)), dma((n_voc,)),
            dma((8,)),
        ],
        compiler_params=pltpu.CompilerParams(
            collective_id=0, has_side_effects=True, vmem_limit_bytes=40 << 20
        ),
        name="gather_and_softmax",
    )(
        *[pltpu.with_memory_space_constraint(a, pltpu.HBM) for a in (
            student_hidden, teacher_rows, student_head, teacher_head,
            lengths, line(route), line(sampled_ids), line(mix_flags),
        )]
    )
    grad, div = pl.pallas_call(
        functools.partial(grad_kernel, n_tok),
        out_shape=(
            jax.ShapeDtypeStruct((ds, cols), BF16),
            jax.ShapeDtypeStruct((1, grp), F32),
        ),
        in_specs=[vmem] * 3,
        out_specs=(hbm, vmem),
        scratch_shapes=[pltpu.VMEM((n_voc, fs, cols), BF16), dma((n_voc,))],
        compiler_params=pltpu.CompilerParams(vmem_limit_bytes=12 << 20),
        name="head_grad",
    )(rows_t, dl, div_all)
    return div.reshape(grp), grad


def solution(mesh):
    in_specs = (
        P("tok", "voc"),
        P("tok", "voc"),
        P(None, ("tok", "voc")),
        P(None, ("tok", "voc")),
        P(),
        P(),
        P(),
        P(),
    )
    out_specs = (P("tok"), P(None, ("tok", "voc")))
    body = functools.partial(on_device, mesh.shape["tok"], mesh.shape["voc"])
    return jax.shard_map(body, mesh=mesh, in_specs=in_specs, out_specs=out_specs, check_vma=False)
```

```python
import functools
import math

import jax
import jax.numpy as jnp
from jax import lax
from jax.experimental import pallas as pl
from jax.experimental.pallas import tpu as pltpu
from jax.sharding import PartitionSpec as P

MESH = pl.DeviceIdType.MESH
F32 = jnp.float32
BF16 = jnp.bfloat16


def grid_of(n_tok):
    cores = 2 if n_tok % 2 == 0 else 1
    chips = n_tok // cores
    wide = math.isqrt(chips)
    while chips % wide:
        wide -= 1
    return chips // wide, wide, cores


def partner(me, step, count):
    if count & (count - 1):
        return lax.rem(me + step, count)
    out = me
    bit = 1
    while bit < count:
        if step & bit:
            out = out + bit - 2 * bit * lax.rem(out // bit, 2)
        bit *= 2
    return out


def merge(block):
    row = lambda q: block[:, q:q + 1, :]
    ms, zs, mu, zu, acc, ps, pu = [row(q) for q in range(7)]
    top_s, top_u = jnp.max(ms, axis=0), jnp.max(mu, axis=0)
    ds, du = ms - top_s[None], mu - top_u[None]
    es = jnp.exp(ds)
    return (
        top_s,
        jnp.sum(zs * es, axis=0),
        top_u,
        jnp.sum(zu * jnp.exp(du), axis=0),
        jnp.sum(es * (acc + zs * (ds - du)), axis=0),
        jnp.sum(ps, axis=0),
        jnp.sum(pu, axis=0),
    )


def gather_kernel(
    n_tok, n_voc, hs, ht, ws, wt, lengths_in, route_in, ids_in, flags_in,
    rows_t_out, dl_out, div_out,
    lengths, route, ids, flags, buf, hs_v, ht_v, vs, vt, stat1, stat2,
    send_z, recv_z, send_a, recv_a, send_b, recv_b, send_d, send_c, recv_c,
    send_1, recv_1, send_2, recv_2, loc,
):
    ny, nx, nc = grid_of(n_tok)
    tok, voc = lax.axis_index("tok"), lax.axis_index("voc")
    core = lax.rem(tok, nc)
    x = lax.rem(tok // nc, nx)
    y = tok // (nc * nx)
    tok_of = lambda yy, xx, cc: (yy * nx + xx) * nc + cc
    grp = hs.shape[0]
    tokens = grp * n_tok
    cols = ws.shape[1]
    fs, ft = hs.shape[1], ht.shape[1]
    first_col = (tok * n_voc + voc) * cols

    own = [
        pltpu.make_async_copy(hs, hs_v, loc.at[0]),
        pltpu.make_async_copy(ht, ht_v, loc.at[1]),
        pltpu.make_async_copy(ws, vs, loc.at[2]),
        pltpu.make_async_copy(wt, vt, loc.at[3]),
        pltpu.make_async_copy(lengths_in, lengths, loc.at[4]),
        pltpu.make_async_copy(route_in, route, loc.at[5]),
        pltpu.make_async_copy(ids_in, ids, loc.at[6]),
        pltpu.make_async_copy(flags_in, flags, loc.at[7]),
    ]
    for copy in own:
        copy.start()

    barrier = pltpu.get_barrier_semaphore()
    for i in range(1, n_tok):
        pl.semaphore_signal(
            barrier, inc=1, device_id=(lax.rem(tok + i, n_tok), voc), device_id_type=MESH
        )
    for j in range(1, n_voc):
        pl.semaphore_signal(
            barrier, inc=1, device_id=(tok, partner(voc, j, n_voc)), device_id_type=MESH
        )
    for copy in own[:2]:
        copy.wait()
    buf[voc, y, x, core, :, :ft] = ht_v[...]
    buf[voc, y, x, core, :, ft:] = hs_v[...]
    pl.semaphore_wait(barrier, n_tok + n_voc - 2)

    started = []

    def push(src, dst, ssem, rsem, device):
        copy = pltpu.make_async_remote_copy(
            src_ref=src, dst_ref=dst, send_sem=ssem, recv_sem=rsem,
            device_id=device, device_id_type=MESH,
        )
        copy.start()
        started.append(copy)

    def arrived(dst, ssem, rsem, device):
        pltpu.make_async_remote_copy(
            src_ref=dst, dst_ref=dst, send_sem=ssem, recv_sem=rsem,
            device_id=device, device_id_type=MESH,
        ).wait_recv()

    def send_along_z(j):
        to = partner(voc, j, n_voc)
        block = buf.at[voc, y, x, core]
        push(block, block, send_z.at[to], recv_z.at[voc], (tok, to))

    def wait_along_z(j):
        k = partner(voc, j, n_voc)
        arrived(buf.at[k, y, x, core], send_z.at[k], recv_z.at[k], (tok, k))

    sides = ((nx, ny), (ny, nx))
    mine_at = ((x, y), (y, x))
    direct = lambda j: j == n_voc - 1

    def place(o, a, b):
        return (b, a) if o == 0 else (a, b)

    def block_at(o, k, a, b):
        yy, xx = place(o, a, b)
        return buf.at[k, yy, xx, core]

    def device(o, a, b):
        yy, xx = place(o, a, b)
        return (tok_of(yy, xx, core), voc)

    def second_axis(o, k, a):
        b = mine_at[o][1]
        for i in range(1, sides[o][1]):
            to = lax.rem(b + i, sides[o][1])
            push(block_at(o, k, a, b), block_at(o, k, a, b), send_b.at[k, to, a],
                 recv_b.at[k, b, a], device(o, mine_at[o][0], to))

    def first_hop(j):
        k, o = partner(voc, j, n_voc), j % 2
        a, b = mine_at[o]
        block = block_at(o, k, a, b)
        if direct(j):
            for i in range(1, sides[o][0]):
                for n in range(1, sides[o][1]):
                    to_a, to_b = lax.rem(a + i, sides[o][0]), lax.rem(b + n, sides[o][1])
                    push(block, block, send_d.at[to_a, to_b], recv_b.at[k, b, a],
                         device(o, to_a, to_b))
        for i in range(1, sides[o][0]):
            to = lax.rem(a + i, sides[o][0])
            push(block, block, send_a.at[k, to], recv_a.at[k, a], device(o, to, b))
        second_axis(o, k, a)

    def second_hop(j):
        k, o = partner(voc, j, n_voc), j % 2
        a, b = mine_at[o]
        for i in range(1, sides[o][0]):
            at = lax.rem(a + i, sides[o][0])
            arrived(block_at(o, k, at, b), send_a.at[k, at], recv_a.at[k, at], device(o, at, b))
            if not direct(j):
                second_axis(o, k, at)

    def core_hop(j):
        k, o = partner(voc, j, n_voc), j % 2
        a, b = mine_at[o]
        for i in range(1, sides[o][1]):
            at = lax.rem(b + i, sides[o][1])
            for n in range(sides[o][0]):
                arrived(block_at(o, k, n, at), send_b.at[k, at, n], recv_b.at[k, at, n],
                        device(o, a, at))
        for i in range(1, nc):
            to = lax.rem(core + i, nc)
            push(buf.at[k, :, :, core], buf.at[k, :, :, core],
                 send_c.at[k], recv_c.at[k], (tok_of(y, x, to), voc))

    def wait_core(j):
        k = partner(voc, j, n_voc)
        for i in range(1, nc):
            cc = lax.rem(core + i, nc)
            arrived(buf.at[k, :, :, cc], send_c.at[k], recv_c.at[k], (tok_of(y, x, cc), voc))

    def product(j):
        k = partner(voc, j, n_voc)
        out = []
        for first, depth, head in ((0, ft, vt), (ft, fs, vs)):
            rows = buf[k, :, :, :, :, first:first + depth].reshape(tokens, depth)
            part = head[pl.ds(pl.multiple_of(k * depth, depth), depth), :]
            out.append(jnp.dot(rows, part, preferred_element_type=F32))
        return out

    def features_first(j):
        k = partner(voc, j, n_voc)
        rows_t_out[k] = buf[k, :, :, :, :, ft:].reshape(tokens, fs).T

    u = jnp.zeros((tokens, cols), F32)
    s = jnp.zeros((tokens, cols), F32)
    for j in range(n_voc + 3):
        if j == 0:
            for i in range(1, min(3, n_voc)):
                send_along_z(i)
            first_hop(0)
        elif j < n_voc:
            wait_along_z(j)
            if j + 2 < n_voc:
                send_along_z(j + 2)
            first_hop(j)
        if 0 <= j - 1 < n_voc:
            second_hop(j - 1)
        if 0 <= j - 2 < n_voc:
            core_hop(j - 2)
        if 0 <= j - 3 < n_voc:
            wait_core(j - 3)
            if j == 3:
                for copy in own[2:]:
                    copy.wait()
            du, ds = product(j - 3)
            u = u + du
            s = s + ds
            if j - 3 < n_voc - 1:
                features_first(j - 3)

    perm = (lax.broadcasted_iota(jnp.int32, (tokens, tokens), 0) == route[...]).astype(BF16)
    hi = u.astype(BF16)
    rest = u - hi.astype(F32)
    mid = rest.astype(BF16)
    low = (rest - mid.astype(F32)).astype(BF16)
    move = lambda part: jnp.dot(perm, part, preferred_element_type=F32)
    u = (move(hi) + move(mid)) + move(low)
    s, u = s.T, u.T

    entry = lax.broadcasted_iota(jnp.int32, (cols, tokens), 0) + first_col
    picked = entry == ids[...]
    ms = jnp.max(s, axis=0, keepdims=True)
    mu = jnp.max(u, axis=0, keepdims=True)
    cs, cu = s - ms, u - mu
    es = jnp.exp(cs)
    total = lambda a: jnp.sum(a, axis=0, keepdims=True)
    mine = (
        ms, total(es), mu, total(jnp.exp(cu)), total(es * (cs - cu)),
        total(jnp.where(picked, s, 0.0)), total(jnp.where(picked, u, 0.0)),
    )

    def put(slots, at, values):
        for q, value in enumerate(values):
            slots[at, q:q + 1, :] = value
        slots[at, 7:8, :] = jnp.zeros_like(values[0])

    put(stat1, tok, mine)
    for i in range(1, n_tok):
        to = lax.rem(tok + i, n_tok)
        push(stat1.at[tok], stat1.at[tok], send_1.at[to], recv_1.at[tok], (to, voc))

    features_first(n_voc - 1)

    for i in range(1, n_tok):
        at = lax.rem(tok + i, n_tok)
        arrived(stat1.at[at], send_1.at[at], recv_1.at[at], (at, voc))
    put(stat2, voc, merge(stat1[...]))
    for j in range(1, n_voc):
        to = partner(voc, j, n_voc)
        push(stat2.at[voc], stat2.at[voc], send_2.at[to], recv_2.at[voc], (tok, to))
    position = lax.broadcasted_iota(jnp.int32, (1, tokens), 1)
    limit = jnp.zeros((1, tokens), jnp.int32)
    for w in range(n_tok):
        limit = jnp.where(position // grp == w, lengths[w], limit)
    live = (lax.rem(position, grp) < limit).astype(F32)
    for j in range(1, n_voc):
        at = partner(voc, j, n_voc)
        arrived(stat2.at[at], send_2.at[at], recv_2.at[at], (tok, at))
    ms, zs, mu, zu, acc, ps, pu = merge(stat2[...])
    log_zs, log_zu = jnp.log(zs), jnp.log(zu)
    kl = acc / zs - log_zs + log_zu
    mixed = 1.0 / (0.2 * jnp.exp((pu - mu - log_zu) - (ps - ms - log_zs)) + 0.8)
    weight = jnp.where(flags[...] == 1, mixed, 1.0)
    ls = s - ms - log_zs
    gap = ls - (u - mu - log_zu)
    dl = (live * weight) * jnp.exp(ls) * (gap - kl)
    dl_out[...] = dl.T.astype(BF16)
    div_out[...] = live * kl
    for copy in started:
        copy.wait_send()


def grad_kernel(n_tok, rows_t, dl, div_all, grad, div, made, sems):
    n_voc, fs, tokens = rows_t.shape
    copies = []
    for k in range(n_voc):
        made[k] = jnp.dot(rows_t[k], dl[...], preferred_element_type=F32).astype(BF16)
        copies.append(pltpu.make_async_copy(made.at[k], grad.at[pl.ds(k * fs, fs)], sems.at[k]))
        copies[-1].start()
    grp = tokens // n_tok
    shift = lax.rem(tokens - lax.axis_index("tok") * grp, tokens)
    turned = pltpu.roll(jnp.broadcast_to(div_all[...], (8, tokens)), shift, 1)
    div[...] = turned[0:1, :grp]
    for copy in copies:
        copy.wait()


def on_device(
    n_tok, n_voc, student_hidden, teacher_rows, student_head, teacher_head,
    lengths, route, sampled_ids, mix_flags,
):
    grp, fs = student_hidden.shape
    ft = teacher_rows.shape[1]
    tokens = grp * n_tok
    ds, cols = student_head.shape
    dt = teacher_head.shape[0]
    ny, nx, nc = grid_of(n_tok)
    side = max(nx, ny)
    dma = pltpu.SemaphoreType.DMA
    hbm = pl.BlockSpec(memory_space=pltpu.HBM)
    vmem = pl.BlockSpec(memory_space=pltpu.VMEM)
    line = lambda a: a.reshape(1, tokens)
    rows_t, dl, div_all = pl.pallas_call(
        functools.partial(gather_kernel, n_tok, n_voc),
        out_shape=(
            jax.ShapeDtypeStruct((n_voc, fs, tokens), BF16),
            jax.ShapeDtypeStruct((tokens, cols), BF16),
            jax.ShapeDtypeStruct((1, tokens), F32),
        ),
        in_specs=[hbm] * 8,
        out_specs=(vmem, vmem, vmem),
        scratch_shapes=[
            pltpu.SMEM(lengths.shape, jnp.int32),
            pltpu.VMEM((1, tokens), jnp.int32),
            pltpu.VMEM((1, tokens), jnp.int32),
            pltpu.VMEM((1, tokens), jnp.int32),
            pltpu.VMEM((n_voc, ny, nx, nc, grp, ft + fs), BF16),
            pltpu.VMEM((grp, fs), BF16),
            pltpu.VMEM((grp, ft), BF16),
            pltpu.VMEM((ds, cols), BF16),
            pltpu.VMEM((dt, cols), BF16),
            pltpu.VMEM((n_tok, 8, tokens), F32),
            pltpu.VMEM((n_voc, 8, tokens), F32),
            dma((n_voc,)), dma((n_voc,)),
            dma((n_voc, side)), dma((n_voc, side)),
            dma((n_voc, side, side)), dma((n_voc, side, side)),
            dma((side, side)),
            dma((n_voc,)), dma((n_voc,)),
            dma((n_tok,)), dma((n_tok,)),
            dma((n_voc,)), dma((n_voc,)),
            dma((8,)),
        ],
        compiler_params=pltpu.CompilerParams(
            collective_id=0, has_side_effects=True, vmem_limit_bytes=40 << 20
        ),
        name="gather_and_softmax",
    )(
        *[pltpu.with_memory_space_constraint(a, pltpu.HBM) for a in (
            student_hidden, teacher_rows, student_head, teacher_head,
            lengths, line(route), line(sampled_ids), line(mix_flags),
        )]
    )
    grad, div = pl.pallas_call(
        functools.partial(grad_kernel, n_tok),
        out_shape=(
            jax.ShapeDtypeStruct((ds, cols), BF16),
            jax.ShapeDtypeStruct((1, grp), F32),
        ),
        in_specs=[vmem] * 3,
        out_specs=(hbm, vmem),
        scratch_shapes=[pltpu.VMEM((n_voc, fs, cols), BF16), dma((n_voc,))],
        compiler_params=pltpu.CompilerParams(vmem_limit_bytes=12 << 20),
        name="head_grad",
    )(rows_t, dl, div_all)
    return div.reshape(grp), grad


def solution(mesh):
    in_specs = (
        P("tok", "voc"),
        P("tok", "voc"),
        P(None, ("tok", "voc")),
        P(None, ("tok", "voc")),
        P(),
        P(),
        P(),
        P(),
    )
    out_specs = (P("tok"), P(None, ("tok", "voc")))
    body = functools.partial(on_device, mesh.shape["tok"], mesh.shape["voc"])
    return jax.shard_map(body, mesh=mesh, in_specs=in_specs, out_specs=out_specs, check_vma=False)
```
